128 devices in a mesh: retr: 8 (over y, core), store: 16 (over x, z).
Axes of the slice: x: 4, y: 4, z: 4, core: 2. Of those that a mesh axis runs over, the one named last changes fastest.
Arguments:
- tokens: bfloat16 [4096, 8192], P('retr', 'store'), may hold values from -6 to 6
- norm_gain: float32 [8192], replicated, may hold values from 0.1 to 1.9
- query_weight: bfloat16 [8192, 8192], P(None, 'store'), may hold values from -1 to 1
- kv_weight: bfloat16 [896, 2, 8192], P('store'), may hold values from -4 to 4
- out_weight: bfloat16 [8192, 8192], P('store'), may hold values from -0.0625 to 0.0625
- neighbour_pool: bfloat16 [128, 128, 896], P('retr'), may hold values from -6 to 6
- neighbour_shard: int32 [64, 2], P('retr'), may hold values from 0 to 7, all different within a row; in each aligned block of 8 rows (0 to 7, 8 to 15, ...) at most 2 rows name the same one
- neighbour_slot: int32 [64, 2], P('retr'), may hold values from 0 to 15
Outputs:
- mixed: bfloat16 [4096, 8192], P('retr', 'store')
The draws below stay inside these ranges and needn't reach their ends.
Inputs may be any that keep to these rules, and one draw needn't show every extreme that they name: `neighbour_shard`: the 2 neighbours of a span lie on different shards. Among the 8 spans of one aligned block (the spans of one index of retr), no shard is named more than 2 times, and in some block one shard is named exactly 2 times.
All inputs are finite; a program needn't handle non-finite values.
Results may differ from the reference program's by a relative error of at most 0.0095.
Values may be sent and summed in bfloat16 or wider, within the bound.
A program may use at most 192 MiB of HBM per device.

```python
import math
import jax
import jax.numpy as jnp
import numpy as np
from jax import lax

D = 8192
H = 64
DH = 128
ENC = 896
SPAN = 64
NL = 128
NEIGH = 2
SLOTS = 16
CH_DEV = 8
CAP = 2
TOKENS = 4096
SPANS = 64
POOL = 128
N_RETR = 8
N_STORE = 16


def draw_query_weight(key, part):
    key = jax.random.fold_in(key, 11)
    first = jax.random.fold_in(key, 0)
    weight = jnp.clip(jax.random.normal(first, (D, H * DH), jnp.float32), -6.0, 6.0) * D ** (-0.5)
    return weight.astype(jnp.bfloat16)


def draw_kv_weight(key, part):
    key = jax.random.fold_in(key, 12)
    weight = jnp.clip(jax.random.normal(key, (ENC, 2, H * DH), jnp.float32), -6.0, 6.0) * ENC ** (-0.5)
    return weight.astype(jnp.bfloat16)


def draw_neighbour_pool(key, part):
    key = jax.random.fold_in(key, 13)
    first = jax.random.fold_in(key, 0)
    pool = jax.random.truncated_normal(first, -6.0, 6.0, (POOL, NL, ENC), jnp.float32)
    return pool.astype(jnp.bfloat16)


def set_ends(values, key, least, largest):
    extent = values.shape
    place = [jax.random.randint(jax.random.fold_in(key, axis), (), 0, extent[axis]) for axis in range(len(extent))]
    values = values.at[tuple(place)].set(least)
    longest = extent.index(max(extent))
    place[longest] = (place[longest] + 1) % extent[longest]
    return values.at[tuple(place)].set(largest)


def levels(rng, dims, cuts, least, top_value):
    factor_of, own = 1.0, jax.random.fold_in(rng, 6)
    for axis_at, shards_of in cuts:
        draws = jnp.exp(jax.random.uniform(jax.random.fold_in(own, axis_at), (shards_of,), jnp.float32, least / len(cuts), top_value / len(cuts)))
        factor_of = factor_of * jnp.repeat(draws, dims[axis_at] // shards_of).reshape([-1 if axis == axis_at else 1 for axis in range(len(dims))])
    return factor_of


def shared_out(own_key, own, number, rows, count, top, reach, lean):
    ranking = jax.random.permutation(own_key, count)
    crowded, usual = portions_of(count, rows * top, reach, lean, True), portions_of(count, rows * top, reach, lean, False)
    places = jnp.arange(count)

    def named(lengths, offset_by):
        used = int((lengths > 0).sum())
        fixed = max(1, used // 4)
        shifted = fixed + (places - fixed + offset_by * (used - fixed)) % max(1, count - fixed)
        return jnp.zeros((count,), jnp.int32).at[ranking[jnp.where(places < fixed, places, shifted)]].set(jnp.asarray(lengths, jnp.int32))

    lengths = jnp.where(number % 4 == 0, named(crowded, number // 4), named(usual, number - number // 4 - 1))
    mixed = jax.random.permutation(jax.random.fold_in(own, 3), count)
    source_of, receiver = mixed[0:count // 2 * 2:2], mixed[1:count // 2 * 2:2]
    room = jnp.minimum(lengths[source_of] - 1, reach - lengths[receiver]) // 2
    room = jnp.where((source_of == ranking[0]) | (receiver == ranking[0]) | (lengths[receiver] == 0), 0, jnp.maximum(room, 0))
    shifted = jax.random.randint(jax.random.fold_in(own, 4), (count // 2,), 0, 1 << 20) % (room + 1)
    lengths = lengths.at[source_of].add(-shifted).at[receiver].add(shifted)
    labels = jnp.searchsorted(jnp.cumsum(lengths), jnp.arange(rows * top), side="right").astype(jnp.int32)
    listing = labels.reshape(top, rows).T
    listing = listing[jax.random.permutation(jax.random.fold_in(own, 1), rows)]
    offset_by = jax.random.randint(jax.random.fold_in(own, 2), (rows, 1), 0, top)
    return jnp.take_along_axis(listing, (jnp.arange(top)[None, :] + offset_by) % top, axis=1)


def portions_of(amount, total, reach, slope, full):
    portions = [(1 << 20) // math.isqrt(grade ** slope) + 1 for grade in range(1, amount + 1)]
    largest = reach if full else min(reach, max(-(-total // amount), total * portions[0] // sum(portions)))
    least = 1 if total - largest >= amount - 1 else 0
    holding, surplus = [largest] + [least] * (amount - 1), total - largest - least * (amount - 1)
    while surplus > 0:
        free = [i for i in range(1, amount) if holding[i] < largest] or [i for i in range(1, amount) if holding[i] < reach]
        mass, remaining = sum([portions[i] for i in free]), surplus
        for i in free:
            extra = min(reach - holding[i], max(1, remaining * portions[i] // mass), surplus)
            holding[i] = holding[i] + extra
            surplus = surplus - extra
    return np.array(holding)


def centred(rng, dims, deviation, most, pieces=(), dtype=jnp.bfloat16):
    drawn = jax.random.normal(rng, dims, jnp.float32) * deviation
    if len(pieces) > 0:
        drawn = levels(rng, dims, pieces, -0.22, 0.18) * drawn
    return jnp.clip(drawn, min=-most, max=most).astype(dtype)


def setup_inputs(seed: int = 0) -> dict:
    streams_of = jax.random.split(jax.random.key(seed), 9)
    tokens = centred(streams_of[0], (TOKENS, D), 1.0, 6.0, ((0, 8), (1, 16)))
    norm_gain = jnp.clip(1.0 + 0.18 * jax.random.normal(streams_of[1], (D,), jnp.float32), 0.1, 1.9)
    query_weight = draw_query_weight(jax.random.fold_in(streams_of[8], 71), 0)
    kv_weight = draw_kv_weight(jax.random.fold_in(streams_of[8], 71), 0)
    out_weight = centred(streams_of[4], (H * DH, D), (H * DH) ** -0.5, 0.0625, ((0, 16),))
    neighbour_pool = draw_neighbour_pool(jax.random.fold_in(streams_of[8], 71), 0)
    neighbour_shard_keys = jax.random.split(jax.random.fold_in(streams_of[6], 1), SPANS // CH_DEV)
    neighbour_shard_turns = jax.random.permutation(jax.random.fold_in(streams_of[6], 3), SPANS // CH_DEV)
    neighbour_shard = jax.vmap(lambda own, number: shared_out(jax.random.fold_in(streams_of[6], 2), own, number, CH_DEV, N_RETR, NEIGH, CAP, 2))(neighbour_shard_keys, neighbour_shard_turns).reshape((SPANS, NEIGH))
    neighbour_slot = set_ends(jax.random.randint(streams_of[7], (SPANS, NEIGH), 0, SLOTS), jax.random.fold_in(streams_of[7], 1), 0, SLOTS - 1).astype(jnp.int32)
    return dict(tokens=tokens, norm_gain=norm_gain, query_weight=query_weight, kv_weight=kv_weight, out_weight=out_weight, neighbour_pool=neighbour_pool, neighbour_shard=neighbour_shard, neighbour_slot=neighbour_slot)


def attend_span(item, kv_weight):
    query_rows, context = item
    kv = jnp.dot(context, kv_weight.reshape(ENC, 2 * H * DH), preferred_element_type=jnp.float32).astype(jnp.bfloat16)
    kv = kv.reshape(NEIGH * NL, 2, H, DH)
    keys = kv[:, 0].astype(jnp.float32)
    values = kv[:, 1]
    query = query_rows.reshape(SPAN, H, DH).astype(jnp.float32)
    scores = jnp.einsum('qhd,khd->hqk', query, keys)
    probs = jax.nn.softmax(scores, axis=-1)
    weights = probs.astype(jnp.bfloat16).astype(jnp.float32)
    attended = jnp.einsum('hqk,khd->qhd', weights, values.astype(jnp.float32))
    return attended.reshape(SPAN, H * DH).astype(jnp.bfloat16)

def reference(tokens, norm_gain, query_weight, kv_weight, out_weight, neighbour_pool, neighbour_shard, neighbour_slot):
    xf = tokens.astype(jnp.float32)
    normed = (xf * lax.rsqrt(lax.optimization_barrier(jnp.mean(xf * xf, axis=-1, keepdims=True)) + 1e-05) * norm_gain[None, :]).astype(jnp.bfloat16)
    query = (jnp.dot(normed, query_weight, preferred_element_type=jnp.float32) * DH ** (-0.5)).astype(jnp.bfloat16)
    index = (neighbour_shard * SLOTS + neighbour_slot).astype(jnp.int32).reshape(-1)
    context = neighbour_pool[index].reshape(SPANS, NEIGH * NL, ENC)
    query_spans = query.reshape(SPANS, SPAN, H * DH)
    attended = lax.map(lambda item: attend_span(item, kv_weight), (query_spans, context))
    attended = attended.reshape(TOKENS, H * DH)
    group_width = H // N_STORE * DH
    att_groups = attended.reshape(TOKENS, N_STORE, group_width).transpose(1, 0, 2)
    out_groups = out_weight.reshape(N_STORE, group_width, D)

    def add_group(total, item):
        part_att, part_w = item
        partial_value = jnp.dot(part_att, part_w, preferred_element_type=jnp.float32).astype(jnp.bfloat16)
        partial_value = lax.optimization_barrier(partial_value)
        return (total + partial_value.astype(jnp.float32), None)
    total, _ = lax.scan(add_group, jnp.zeros((TOKENS, D), jnp.float32), (att_groups, out_groups))
    return (xf + total).astype(jnp.bfloat16)
```

```python
import jax
import jax.numpy as jnp
from jax import lax
from jax.experimental import pallas as pl
from jax.experimental.pallas import tpu as pltpu
from jax.sharding import PartitionSpec as P

MESH = pl.DeviceIdType.MESH
BF16, F32, I32 = jnp.bfloat16, jnp.float32, jnp.int32

DH, ENC, SPAN, NL, NEIGH = 128, 896, 64, 128, 2
D, HC, ROWS, HALF, QUART = 8192, 512, 512, 256, 128
EROWS, EPAD = 56, 64
STEP = (0, 1, -1, 2)


def _dot(a, b):
    return jnp.dot(a, b, preferred_element_type=F32)


def kernel(
    tok_ref, gain_ref, shard_ref, slot_ref, wq_hbm, kvw_hbm, wo_hbm, pool_hbm, out_ref,
    slots, wq, acc, ssq, pool, picked, fetched, keys, values, kvraw, kvsend, kvrecv, w32, wkv,
    reqs, table, table_s, place_s, att, wo, send1, recv1h, recv1, send2, recv2h, recv2,
    load_sem, raw_sem, ag_send, ag_recv, req_send, req_recv, kv_send, kv_recv,
    wy_send, wy_recv, pool_send, pool_recv, rs1h_send, rs1h_recv, rs1_send, rs1_recv,
    rs2_send, rs2_recv,
):
    retr, store = lax.axis_index("retr"), lax.axis_index("store")
    x, z = store // 4, store % 4
    y, c = retr // 2, retr % 2

    def device(dx, dy, dz, dc):
        return ((y + dy + 4) % 4 * 2 + (c + dc) % 2, (x + dx + 4) % 4 * 4 + (z + dz + 4) % 4)

    def along(kind, axis, step):
        return device(step, 0, 0, 0) if (kind == 0) == (axis == 1) else device(0, 0, step, 0)

    def column(kind, a, b):
        dx = jnp.where(kind == 0, a, b)
        dz = jnp.where(kind == 0, b, a)
        return (x + dx + 4) % 4 * 4 + (z + dz + 4) % 4

    def offset(i):
        return jnp.where(i == 0, 0, jnp.where(i == 1, 1, jnp.where(i == 2, -1, 2)))

    loads = [
        pltpu.make_async_copy(tok_ref.at[pl.ds(0, HALF)], slots.at[0, 0, 0], load_sem.at[0]),
        pltpu.make_async_copy(tok_ref.at[pl.ds(HALF, HALF)], slots.at[1, 0, 0], load_sem.at[1]),
        pltpu.make_async_copy(pool_hbm, pool, load_sem.at[2]),
        pltpu.make_async_copy(wq_hbm, wq, load_sem.at[3]),
        pltpu.make_async_copy(wo_hbm, wo, load_sem.at[4]),
    ]
    loads[0].start()
    loads[1].start()
    raws = [
        pltpu.make_async_copy(
            kvw_hbm.at[:, :, pl.ds(s * HC + y * DH, DH)], kvraw.at[s], raw_sem.at[s]
        )
        for s in range(16)
    ]
    for copy in raws:
        copy.start()
    for copy in loads[2:]:
        copy.start()

    barrier = pltpu.get_barrier_semaphore()
    for o in range(1, 16):
        pl.semaphore_signal(
            barrier, inc=1, device_id=(retr, (store + o) % 16), device_id_type=MESH
        )
    for o in range(1, 8):
        pl.semaphore_signal(barrier, inc=1, device_id=((retr + o) % 8, store), device_id_type=MESH)
    reqs[...] = jnp.zeros((8, 128), I32)
    reqs[:, 0:2] = shard_ref[...]
    reqs[:, 2:4] = slot_ref[...]
    pl.semaphore_wait(barrier, 22)

    RET = [(o // 2, o % 2) for o in range(8)]
    ORDER = [2, 6, 3, 7, 4, 5, 1]

    def peer_from(o):
        dy, dc = RET[o]
        return (y - dy + 4) % 4 * 2 + (c + dc) % 2

    req_msg = {}
    for o in ORDER:
        req_msg[o] = pltpu.make_async_remote_copy(
            reqs, table.at[retr], req_send.at[o], req_recv.at[o],
            device_id=device(0, RET[o][0], 0, RET[o][1]), device_id_type=MESH,
        )
        req_msg[o].start()

    def gather_msg(k, i, j, h):
        axis = 2 if j else 1
        move = j if j else i
        if move == 3:
            src_move, step, half = (1, -1, 0) if h == 0 else (2, 1, 1)
            src = (i, src_move) if j else (src_move, 0)
            rows = pl.ds(half * QUART, QUART)
            return pltpu.make_async_remote_copy(
                slots.at[k, src[0], src[1], rows], slots.at[k, i, j, rows],
                ag_send.at[k, i, j, h], ag_recv.at[k, i, j, h],
                device_id=along(k, axis, step), device_id_type=MESH,
            )
        src = (i, 0) if j else (0, 0)
        step = -1 if move == 1 else 1
        return pltpu.make_async_remote_copy(
            slots.at[k, src[0], src[1]], slots.at[k, i, j],
            ag_send.at[k, i, j, 0], ag_recv.at[k, i, j, 0],
            device_id=along(k, axis, step), device_id_type=MESH,
        )

    started = []

    def go(k, i, j, h=0):
        msg = gather_msg(k, i, j, h)
        msg.start()
        started.append(msg)

    def came(k, i, j, h=0):
        gather_msg(k, i, j, h).wait_recv()

    loads[0].wait()
    loads[1].wait()
    for k in range(2):
        go(k, 1, 0)
        go(k, 2, 0)
    for k in range(2):
        go(k, 0, 1)
        go(k, 0, 2)

    acc[...] = jnp.zeros((ROWS, HC), F32)
    ssq[...] = jnp.zeros((ROWS, 128), F32)

    def query_block(k, i, j):
        s = column(k, offset(i), offset(j))
        rows = pl.ds(k * HALF, HALF)
        xf = slots[k, i, j].astype(F32)
        sq = xf * xf
        ssq[rows, :] += (sq[:, 0:128] + sq[:, 128:256]) + (sq[:, 256:384] + sq[:, 384:512])
        g4 = gain_ref[s]
        g = jnp.concatenate([g4[t : t + 1, :] for t in range(4)], axis=1)
        acc[rows, :] += _dot((xf * g).astype(BF16), wq[pl.ds(pl.multiple_of(s * HC, HC), HC), :])

    def query_blocks(n, place):
        def body(t, carry):
            i, j = place(t // 2)
            query_block(t % 2, i, j)
            return carry

        lax.fori_loop(0, 2 * n, body, 0)

    for copy in raws:
        copy.wait()

    def split(s, carry):
        raw = kvraw[s].astype(F32)
        one = jnp.where(c == 0, raw[:, 0, :], raw[:, 1, :])
        kvsend[s] = jnp.concatenate([one, jnp.zeros((EPAD - EROWS, DH), F32)], axis=0).astype(BF16)
        return carry

    lax.fori_loop(0, 16, split, 0)
    kv_msg = []
    for o in range(1, 16):
        to = (store + o) % 16
        msg = pltpu.make_async_remote_copy(
            kvsend.at[to], kvrecv.at[store], kv_send.at[o], kv_recv.at[o],
            device_id=(retr, to), device_id_type=MESH,
        )
        msg.start()
        kv_msg.append(msg)
    kvrecv[store] = kvsend[store]

    table[retr] = reqs[...]
    for o in ORDER:
        req_msg[o].wait_recv()
    to_smem = pltpu.make_async_copy(table, table_s, load_sem.at[5])
    to_smem.start()
    to_smem.wait()
    loads[2].wait()
    pool_msg = {}
    for o in [*ORDER, 0]:
        dy, dc = RET[o]
        to = (y + dy) % 4 * 2 + (c + dc) % 2
        first, second, seen = I32(0), I32(0), I32(0)
        for n in range(16):
            hit = table_s[to, n // 2, n % 2] == retr
            slot = table_s[to, n // 2, 2 + n % 2]
            first = jnp.where(hit & (seen == 0), slot, first)
            second = jnp.where(hit & (seen == 1), slot, second)
            seen = seen + jnp.where(hit, 1, 0)
        if o == 0:
            fetched[2 * retr] = pool[first]
            fetched[2 * retr + 1] = pool[second]
            continue
        picked[2 * o] = pool[first]
        picked[2 * o + 1] = pool[second]
        pool_msg[o] = pltpu.make_async_remote_copy(
            picked.at[pl.ds(2 * o, 2)], fetched.at[pl.ds(2 * retr, 2)],
            pool_send.at[o], pool_recv.at[o],
            device_id=device(0, dy, 0, dc), device_id_type=MESH,
        )
        pool_msg[o].start()
    mine = [table_s[retr, n // 2, n % 2] for n in range(16)]
    for n in range(16):
        before = I32(0)
        for m in range(n):
            before = before + jnp.where(mine[m] == mine[n], 1, 0)
        place_s[n] = 2 * mine[n] + before

    loads[3].wait()
    query_blocks(1, lambda t: (0, 0))

    for k in range(2):
        came(k, 1, 0)
        go(k, 3, 0, 0)
        go(k, 1, 1)
        go(k, 1, 2)
        came(k, 2, 0)
        go(k, 3, 0, 1)
        go(k, 2, 1)
        go(k, 2, 2)
    query_blocks(2, lambda t: (1 + t, 0))

    for msg in kv_msg:
        msg.wait_recv()

    def assemble(s, carry):
        part = kvrecv[s].astype(F32)
        w32[pl.ds(pl.multiple_of(s * EROWS, 8), EROWS), :] = part[:EROWS]
        return carry

    lax.fori_loop(0, 16, assemble, 0)
    wkv[c, :, pl.ds(pl.multiple_of(y * DH, DH), DH)] = w32[...].astype(BF16)

    def weight_part(dy, dc):
        return wkv.at[(c + dc) % 2, :, pl.ds(pl.multiple_of((y - dy + 4) % 4 * DH, DH), DH)]

    def weight_msg(o):
        dy, dc = RET[o]
        if dc:
            return pltpu.make_async_remote_copy(
                weight_part(dy, 0), weight_part(dy, 0), wy_send.at[o], wy_recv.at[o],
                device_id=device(0, 0, 0, 1), device_id_type=MESH,
            )
        return pltpu.make_async_remote_copy(
            weight_part(0, 0), weight_part(0, 0), wy_send.at[o], wy_recv.at[o],
            device_id=device(0, dy, 0, 0), device_id_type=MESH,
        )

    wy_msg = {}

    def weight_go(o):
        wy_msg[o] = weight_msg(o)
        wy_msg[o].start()

    for o in (2, 6, 4, 1):
        weight_go(o)

    for k in range(2):
        came(k, 0, 1)
        go(k, 0, 3, 0)
        came(k, 0, 2)
        go(k, 0, 3, 1)
    query_blocks(2, lambda t: (0, 1 + t))
    for k in range(2):
        came(k, 3, 0, 0)
        came(k, 3, 0, 1)
        go(k, 3, 1)
        go(k, 3, 2)
    query_blocks(1, lambda t: (3, 0))
    for i in (1, 2):
        for k in range(2):
            came(k, i, 1)
            go(k, i, 3, 0)
            came(k, i, 2)
            go(k, i, 3, 1)
    query_blocks(4, lambda t: (1 + t // 2, 1 + t % 2))

    for o in (2, 6, 4):
        wy_msg[o].wait_recv()
        weight_go(o + 1)

    def kv_block(r):
        ctx = fetched[pl.ds(2 * r, 2)].reshape(2 * NL, ENC)
        keys[pl.ds(2 * r, 2)] = _dot(ctx, wkv[0]).astype(BF16).reshape(2, NL, HC)
        values[pl.ds(2 * r, 2)] = _dot(ctx, wkv[1]).astype(BF16).reshape(2, NL, HC)

    for k in range(2):
        came(k, 3, 1)
        go(k, 3, 3, 0)
        came(k, 3, 2)
        go(k, 3, 3, 1)
    query_blocks(2, lambda t: (3, 1 + t))
    for o in (1, 3, 5, 7):
        wy_msg[o].wait_recv()
    pool_msg[1].wait_recv()
    first_two = (retr, peer_from(1))
    lax.fori_loop(
        0, 2, lambda t, v: (kv_block(jnp.where(t == 0, first_two[0], first_two[1])), v)[1], 0
    )
    for k in range(2):
        for i in range(4):
            came(k, i, 3, 0)
            came(k, i, 3, 1)
    query_blocks(4, lambda t: (t, 3))
    for group in ((2, 6), (3, 7), (4, 5)):
        for o in group:
            pool_msg[o].wait_recv()
        pair = tuple(peer_from(o) for o in group)
        lax.fori_loop(
            0, 2, lambda t, v: (kv_block(jnp.where(t == 0, pair[0], pair[1])), v)[1], 0
        )

    def span(n, carry):
        rows = pl.ds(pl.multiple_of(n * SPAN, SPAN), SPAN)
        mean = jnp.sum(ssq[rows, :], axis=1, keepdims=True) * (1.0 / D)
        q = (acc[rows, :] * (lax.rsqrt(mean + 1e-05) * DH**-0.5)).astype(BF16)
        j0, j1 = place_s[2 * n], place_s[2 * n + 1]
        ks = jnp.concatenate([keys[j0], keys[j1]], axis=0)
        vs = jnp.concatenate([values[j0], values[j1]], axis=0)
        outs = []
        for h in range(4):
            cols = slice(h * DH, (h + 1) * DH)
            sc = lax.dot_general(
                q[:, cols], ks[:, cols], (((1,), (1,)), ((), ())), preferred_element_type=F32
            )
            e = jnp.exp(sc - jnp.max(sc, axis=1, keepdims=True))
            w = (e / jnp.sum(e, axis=1, keepdims=True)).astype(BF16)
            outs.append(_dot(w, vs[:, cols]).astype(BF16))
        att[rows, :] = jnp.concatenate(outs, axis=1)
        return carry

    lax.fori_loop(0, 8, span, 0)

    loads[4].wait()

    def block(k, a, b):
        s = column(k, a, b)
        return _dot(
            att[pl.ds(pl.multiple_of(k * HALF, HALF), HALF), :],
            wo[:, pl.ds(pl.multiple_of(s * HC, HC), HC)],
        )

    def one_h(k, i, h):
        return pltpu.make_async_remote_copy(
            send1.at[k, i, 0, pl.ds(h * QUART, QUART)], recv1h.at[k, i, h],
            rs1h_send.at[k, i, h], rs1h_recv.at[k, i, h],
            device_id=along(k, 2, 1 if h == 0 else -1), device_id_type=MESH,
        )

    def one(k, i, d):
        return pltpu.make_async_remote_copy(
            send1.at[k, i, 1 + d], recv1.at[k, i, d], rs1_send.at[k, i, d], rs1_recv.at[k, i, d],
            device_id=along(k, 2, 1 if d == 0 else -1), device_id_type=MESH,
        )

    def two_h(k, h):
        return pltpu.make_async_remote_copy(
            send2.at[k, 0, pl.ds(h * QUART, QUART)], recv2h.at[k, h],
            rs2_send.at[k, h], rs2_recv.at[k, h],
            device_id=along(k, 1, 1 if h == 0 else -1), device_id_type=MESH,
        )

    def two(k, d):
        return pltpu.make_async_remote_copy(
            send2.at[k, 1 + d], recv2.at[k, d], rs2_send.at[k, 2 + d], rs2_recv.at[k, 2 + d],
            device_id=along(k, 1, 1 if d == 0 else -1), device_id_type=MESH,
        )

    FAR = (3, 1, 2, 0)
    for i in FAR:
        for k in range(2):
            send1[k, i, 0] = block(k, STEP[i], 2).astype(BF16)
            for h in range(2):
                one_h(k, i, h).start()
    for i in FAR:
        for k in range(2):
            for d in range(2):
                one_h(k, i, d).wait_recv()
                part = block(k, STEP[i], 1 if d == 0 else -1)
                at = pl.ds(d * QUART, QUART)
                rest = pl.ds((1 - d) * QUART, QUART)
                got = recv1h[k, i, d].astype(F32)
                send1[k, i, 1 + d, at] = (part[d * QUART : (d + 1) * QUART] + got).astype(BF16)
                send1[k, i, 1 + d, rest] = part[(1 - d) * QUART : (2 - d) * QUART].astype(BF16)
                one(k, i, d).start()
    for i in FAR:
        for k in range(2):
            for d in range(2):
                one(k, i, d).wait_recv()
            total = block(k, STEP[i], 0) + recv1[k, i, 0].astype(F32) + recv1[k, i, 1].astype(F32)
            if i == 3:
                send2[k, 0] = total.astype(BF16)
                for h in range(2):
                    two_h(k, h).start()
            elif i:
                d = i - 1
                two_h(k, d).wait_recv()
                at = pl.ds(d * QUART, QUART)
                rest = pl.ds((1 - d) * QUART, QUART)
                got = recv2h[k, d].astype(F32)
                send2[k, 1 + d, at] = (total[d * QUART : (d + 1) * QUART] + got).astype(BF16)
                send2[k, 1 + d, rest] = total[(1 - d) * QUART : (2 - d) * QUART].astype(BF16)
                two(k, d).start()
            else:
                for d in range(2):
                    two(k, d).wait_recv()
                total = total + recv2[k, 0].astype(F32) + recv2[k, 1].astype(F32)
                own = slots[k, 0, 0].astype(F32)
                out_ref[pl.ds(k * HALF, HALF), :] = (own + total).astype(BF16)

    for msg in started:
        msg.wait_send()
    for msg in kv_msg:
        msg.wait_send()
    for o in ORDER:
        req_msg[o].wait_send()
        pool_msg[o].wait_send()
        wy_msg[o].wait_send()
    for k in range(2):
        for i in range(4):
            for d in range(2):
                one_h(k, i, d).wait_send()
                one(k, i, d).wait_send()
        for d in range(2):
            two_h(k, d).wait_send()
            two(k, d).wait_send()


def on_device(
    tokens, norm_gain, query_weight, kv_weight, out_weight, neighbour_pool, neighbour_shard, neighbour_slot
):
    gain = norm_gain.reshape(16, 4, 128)
    vmem, hbm = pl.BlockSpec(memory_space=pltpu.VMEM), pl.BlockSpec(memory_space=pl.ANY)
    dma = pltpu.SemaphoreType.DMA
    return pl.pallas_call(
        kernel,
        out_shape=jax.ShapeDtypeStruct((ROWS, HC), BF16),
        in_specs=[hbm, vmem, vmem, vmem, hbm, hbm, hbm, hbm],
        out_specs=vmem,
        scratch_shapes=[
            pltpu.VMEM((2, 4, 4, HALF, HC), BF16),
            pltpu.VMEM((D, HC), BF16),
            pltpu.VMEM((ROWS, HC), F32),
            pltpu.VMEM((ROWS, 128), F32),
            pltpu.VMEM((16, NL, ENC), BF16),
            pltpu.VMEM((16, NL, ENC), BF16),
            pltpu.VMEM((16, NL, ENC), BF16),
            pltpu.VMEM((16, NL, HC), BF16),
            pltpu.VMEM((16, NL, HC), BF16),
            pltpu.VMEM((16, EROWS, 2, DH), BF16),
            pltpu.VMEM((16, EPAD, DH), BF16),
            pltpu.VMEM((16, EPAD, DH), BF16),
            pltpu.VMEM((ENC, DH), F32),
            pltpu.VMEM((2, ENC, HC), BF16),
            pltpu.VMEM((8, 128), I32),
            pltpu.VMEM((8, 8, 128), I32),
            pltpu.SMEM((8, 8, 128), I32),
            pltpu.SMEM((16,), I32),
            pltpu.VMEM((ROWS, HC), BF16),
            pltpu.VMEM((HC, D), BF16),
            pltpu.VMEM((2, 4, 3, HALF, HC), BF16),
            pltpu.VMEM((2, 4, 2, QUART, HC), BF16),
            pltpu.VMEM((2, 4, 2, HALF, HC), BF16),
            pltpu.VMEM((2, 3, HALF, HC), BF16),
            pltpu.VMEM((2, 2, QUART, HC), BF16),
            pltpu.VMEM((2, 2, HALF, HC), BF16),
            dma((6,)), dma((16,)), dma((2, 4, 4, 2)), dma((2, 4, 4, 2)), dma((8,)), dma((8,)),
            dma((16,)), dma((16,)), dma((8,)), dma((8,)), dma((8,)), dma((8,)),
            dma((2, 4, 2)), dma((2, 4, 2)), dma((2, 4, 2)), dma((2, 4, 2)), dma((2, 4)), dma((2, 4)),
        ],
        compiler_params=pltpu.CompilerParams(
            collective_id=0, has_side_effects=True, vmem_limit_bytes=62 << 20
        ),
        cost_estimate=pl.CostEstimate(
            flops=13_000_000_000, bytes_accessed=24_000_000, transcendentals=600_000
        ),
        name="retro_block",
    )(tokens, gain, neighbour_shard, neighbour_slot, query_weight, kv_weight, out_weight, neighbour_pool)


def solution(mesh):
    return jax.shard_map(
        on_device,
        mesh=mesh,
        in_specs=(
            P("retr", "store"),
            P(),
            P(None, "store"),
            P("store", None, None),
            P("store", None),
            P("retr", None, None),
            P("retr", None),
            P("retr", None),
        ),
        out_specs=P("retr", "store"),
        check_vma=False,
    )
```

```python
import jax
import jax.numpy as jnp
from jax import lax
from jax.experimental import pallas as pl
from jax.experimental.pallas import tpu as pltpu
from jax.sharding import PartitionSpec as P

MESH = pl.DeviceIdType.MESH
BF16, F32, I32 = jnp.bfloat16, jnp.float32, jnp.int32

DH, ENC, SPAN, NL, NEIGH = 128, 896, 64, 128, 2
D, HC, ROWS, HALF, QUART = 8192, 512, 512, 256, 128
EROWS, EPAD = 56, 64
STEP = (0, 1, -1, 2)


def _dot(a, b):
    return jnp.dot(a, b, preferred_element_type=F32)


def kernel(
    tok_ref, gain_ref, shard_ref, slot_ref, wq_hbm, kvw_hbm, wo_hbm, pool_hbm, out_ref,
    slots, wq, acc, ssq, pool, picked, fetched, keys, values, kvraw, kvsend, kvrecv, w32, wkv,
    reqs, table, table_s, place_s, att, wo, send1, recv1h, recv1, send2, recv2h, recv2,
    load_sem, raw_sem, ag_send, ag_recv, req_send, req_recv, kv_send, kv_recv,
    wy_send, wy_recv, pool_send, pool_recv, share_send, share_recv, rs1h_send, rs1h_recv, rs1_send, rs1_recv,
    rs2_send, rs2_recv,
):
    retr, store = lax.axis_index("retr"), lax.axis_index("store")
    x, z = store // 4, store % 4
    y, c = retr // 2, retr % 2

    def device(dx, dy, dz, dc):
        return ((y + dy + 4) % 4 * 2 + (c + dc) % 2, (x + dx + 4) % 4 * 4 + (z + dz + 4) % 4)

    def along(kind, axis, step):
        return device(step, 0, 0, 0) if (kind == 0) == (axis == 1) else device(0, 0, step, 0)

    def column(kind, a, b):
        dx = jnp.where(kind == 0, a, b)
        dz = jnp.where(kind == 0, b, a)
        return (x + dx + 4) % 4 * 4 + (z + dz + 4) % 4

    def offset(i):
        return jnp.where(i == 0, 0, jnp.where(i == 1, 1, jnp.where(i == 2, -1, 2)))

    loads = [
        pltpu.make_async_copy(tok_ref.at[pl.ds(0, HALF)], slots.at[0, 0, 0], load_sem.at[0]),
        pltpu.make_async_copy(tok_ref.at[pl.ds(HALF, HALF)], slots.at[1, 0, 0], load_sem.at[1]),
        pltpu.make_async_copy(pool_hbm, pool, load_sem.at[2]),
        pltpu.make_async_copy(wq_hbm, wq, load_sem.at[3]),
        pltpu.make_async_copy(wo_hbm, wo, load_sem.at[4]),
    ]
    loads[0].start()
    loads[1].start()
    raws = [
        pltpu.make_async_copy(
            kvw_hbm.at[:, :, pl.ds(s * HC + y * DH, DH)], kvraw.at[s], raw_sem.at[s]
        )
        for s in range(16)
    ]
    for copy in raws:
        copy.start()
    for copy in loads[2:]:
        copy.start()

    barrier = pltpu.get_barrier_semaphore()
    for o in range(1, 16):
        pl.semaphore_signal(
            barrier, inc=1, device_id=(retr, (store + o) % 16), device_id_type=MESH
        )
    for o in range(1, 8):
        pl.semaphore_signal(barrier, inc=1, device_id=((retr + o) % 8, store), device_id_type=MESH)
    reqs[...] = jnp.zeros((8, 128), I32)
    reqs[0:2, 0:8] = shard_ref[...]
    reqs[2:4, 0:8] = slot_ref[...]

    for copy in raws:
        copy.wait()

    def split(s, carry):
        raw = kvraw[s].astype(F32)
        one = jnp.where(c == 0, raw[:, 0, :], raw[:, 1, :])
        kvsend[s] = jnp.concatenate([one, jnp.zeros((EPAD - EROWS, DH), F32)], axis=0).astype(BF16)
        return carry

    lax.fori_loop(0, 16, split, 0)
    pl.semaphore_wait(barrier, 22)

    RET = [(o // 2, o % 2) for o in range(8)]
    EARLY, LATE = [4, 5, 2, 6], [3, 7, 1]
    ORDER = EARLY + LATE

    def peer_from(o):
        dy, dc = RET[o]
        return (y - dy + 4) % 4 * 2 + (c + dc) % 2

    req_msg = {}
    for o in ORDER:
        req_msg[o] = pltpu.make_async_remote_copy(
            reqs, table.at[retr], req_send.at[o], req_recv.at[o],
            device_id=device(0, RET[o][0], 0, RET[o][1]), device_id_type=MESH,
        )
        req_msg[o].start()

    def gather_msg(k, i, j, h):
        axis = 2 if j else 1
        move = j if j else i
        if move == 3:
            src_move, step, half = (1, -1, 0) if h == 0 else (2, 1, 1)
            src = (i, src_move) if j else (src_move, 0)
            rows = pl.ds(half * QUART, QUART)
            return pltpu.make_async_remote_copy(
                slots.at[k, src[0], src[1], rows], slots.at[k, i, j, rows],
                ag_send.at[k, i, j, h], ag_recv.at[k, i, j, h],
                device_id=along(k, axis, step), device_id_type=MESH,
            )
        src = (i, 0) if j else (0, 0)
        step = -1 if move == 1 else 1
        return pltpu.make_async_remote_copy(
            slots.at[k, src[0], src[1]], slots.at[k, i, j],
            ag_send.at[k, i, j, 0], ag_recv.at[k, i, j, 0],
            device_id=along(k, axis, step), device_id_type=MESH,
        )

    started = []

    def go(k, i, j, h=0):
        msg = gather_msg(k, i, j, h)
        msg.start()
        started.append(msg)

    def came(k, i, j, h=0):
        gather_msg(k, i, j, h).wait_recv()

    loads[0].wait()
    loads[1].wait()
    for k in range(2):
        go(k, 1, 0)
        go(k, 2, 0)
    for k in range(2):
        go(k, 0, 1)
        go(k, 0, 2)

    kv_msg = []
    for o in range(1, 16):
        to = (store + o) % 16
        msg = pltpu.make_async_remote_copy(
            kvsend.at[to], kvrecv.at[store], kv_send.at[o], kv_recv.at[o],
            device_id=(retr, to), device_id_type=MESH,
        )
        msg.start()
        kv_msg.append(msg)
    kvrecv[store] = kvsend[store]

    acc[...] = jnp.zeros((ROWS, HC), F32)
    ssq[...] = jnp.zeros((ROWS, 128), F32)

    def query_block(k, i, j):
        s = column(k, offset(i), offset(j))
        rows = pl.ds(k * HALF, HALF)
        xf = slots[k, i, j].astype(F32)
        sq = xf * xf
        ssq[rows, :] += (sq[:, 0:128] + sq[:, 128:256]) + (sq[:, 256:384] + sq[:, 384:512])
        g4 = gain_ref[s]
        g = jnp.concatenate([g4[t : t + 1, :] for t in range(4)], axis=1)
        acc[rows, :] += _dot((xf * g).astype(BF16), wq[pl.ds(pl.multiple_of(s * HC, HC), HC), :])

    def query_blocks(n, place):
        def body(t, carry):
            i, j = place(t // 2)
            query_block(t % 2, i, j)
            return carry

        lax.fori_loop(0, 2 * n, body, 0)

    table[retr] = reqs[...]
    for o in ORDER:
        req_msg[o].wait_recv()
    to_smem = pltpu.make_async_copy(table, table_s, load_sem.at[5])
    to_smem.start()
    to_smem.wait()
    loads[2].wait()
    def parity(o):
        return (x if o == 4 else z) % 2

    def share_msg(o):
        at = pl.ds(2 * peer_from(o) + parity(o), 1)
        step = 1 - 2 * ((parity(o) + c) % 2)
        return pltpu.make_async_remote_copy(
            fetched.at[at], fetched.at[at], share_send.at[o - 4], share_recv.at[o - 4],
            device_id=device(step, 0, 0, 0) if o == 4 else device(0, 0, step, 0),
            device_id_type=MESH,
        )

    pool_msg = {}
    for o in [*ORDER, 0]:
        dy, dc = RET[o]
        to = (y + dy) % 4 * 2 + (c + dc) % 2
        first, second, seen = I32(0), I32(0), I32(0)
        for n in range(16):
            hit = table_s[to, n % 2, n // 2] == retr
            slot = table_s[to, 2 + n % 2, n // 2]
            first = jnp.where(hit & (seen == 0), slot, first)
            second = jnp.where(hit & (seen == 1), slot, second)
            seen = seen + jnp.where(hit, 1, 0)
        if o == 0:
            fetched[2 * retr] = pool[first]
            fetched[2 * retr + 1] = pool[second]
            continue
        picked[2 * o] = pool[first]
        picked[2 * o + 1] = pool[second]
        n, skip = (1, parity(o)) if dy == 2 else (2, 0)
        pool_msg[o] = pltpu.make_async_remote_copy(
            picked.at[pl.ds(2 * o + skip, n)], fetched.at[pl.ds(2 * retr + skip, n)],
            pool_send.at[o], pool_recv.at[o],
            device_id=device(0, dy, 0, dc), device_id_type=MESH,
        )
        if o in EARLY:
            pool_msg[o].start()
    mine = [table_s[retr, n % 2, n // 2] for n in range(16)]
    for n in range(16):
        before = I32(0)
        for m in range(n):
            before = before + jnp.where(mine[m] == mine[n], 1, 0)
        place_s[n] = 2 * mine[n] + before

    loads[3].wait()
    query_blocks(1, lambda t: (0, 0))

    for k in range(2):
        came(k, 1, 0)
        go(k, 3, 0, 0)
        go(k, 1, 1)
        go(k, 1, 2)
        came(k, 2, 0)
        go(k, 3, 0, 1)
        go(k, 2, 1)
        go(k, 2, 2)
    query_blocks(2, lambda t: (1 + t, 0))

    for msg in kv_msg:
        msg.wait_recv()

    def assemble(s, carry):
        part = kvrecv[s].astype(F32)
        w32[pl.ds(pl.multiple_of(s * EROWS, 8), EROWS), :] = part[:EROWS]
        return carry

    lax.fori_loop(0, 16, assemble, 0)
    wkv[c, :, pl.ds(pl.multiple_of(y * DH, DH), DH)] = w32[...].astype(BF16)

    def weight_part(dy, dc):
        return wkv.at[(c + dc) % 2, :, pl.ds(pl.multiple_of((y - dy + 4) % 4 * DH, DH), DH)]

    def weight_msg(o):
        dy, dc = RET[o]
        if dc:
            return pltpu.make_async_remote_copy(
                weight_part(dy, 0), weight_part(dy, 0), wy_send.at[o], wy_recv.at[o],
                device_id=device(0, 0, 0, 1), device_id_type=MESH,
            )
        return pltpu.make_async_remote_copy(
            weight_part(0, 0), weight_part(0, 0), wy_send.at[o], wy_recv.at[o],
            device_id=device(0, dy, 0, 0), device_id_type=MESH,
        )

    wy_msg = {}

    def weight_go(o):
        wy_msg[o] = weight_msg(o)
        wy_msg[o].start()

    for o in (2, 6, 4, 1):
        weight_go(o)
    for o in LATE:
        pool_msg[o].start()

    for k in range(2):
        came(k, 0, 1)
        go(k, 0, 3, 0)
        came(k, 0, 2)
        go(k, 0, 3, 1)
    query_blocks(2, lambda t: (0, 1 + t))
    for k in range(2):
        came(k, 3, 0, 0)
        came(k, 3, 0, 1)
        go(k, 3, 1)
        go(k, 3, 2)
    query_blocks(1, lambda t: (3, 0))
    for i in (1, 2):
        for k in range(2):
            came(k, i, 1)
            go(k, i, 3, 0)
            came(k, i, 2)
            go(k, i, 3, 1)
    query_blocks(4, lambda t: (1 + t // 2, 1 + t % 2))

    for o in (4, 5):
        pool_msg[o].wait_recv()
        share_msg(o).start()
    for k in range(2):
        came(k, 3, 1)
        go(k, 3, 3, 0)
        came(k, 3, 2)
        go(k, 3, 3, 1)
    query_blocks(2, lambda t: (3, 1 + t))
    for o in (2, 6, 4):
        wy_msg[o].wait_recv()
        weight_go(o + 1)

    def kv_block(r):
        ctx = fetched[pl.ds(2 * r, 2)].reshape(2 * NL, ENC)
        turned = _dot(ctx, wkv[0]).astype(BF16).T
        keys[2 * r] = turned[:, :NL]
        keys[2 * r + 1] = turned[:, NL:]
        values[pl.ds(2 * r, 2)] = _dot(ctx, wkv[1]).astype(BF16).reshape(2, NL, HC)


    def kv_blocks(sources):
        def body(t, carry):
            r = sources[0]
            for n in range(1, len(sources)):
                r = jnp.where(t == n, sources[n], r)
            kv_block(r)
            return carry

        lax.fori_loop(0, len(sources), body, 0)

    for o in (1, 3, 5, 7):
        wy_msg[o].wait_recv()
    for o in (2, 6):
        pool_msg[o].wait_recv()
    kv_blocks((retr, peer_from(2), peer_from(6)))
    for k in range(2):
        for i in range(3):
            came(k, i, 3, 0)
            came(k, i, 3, 1)
    query_blocks(3, lambda t: (t, 3))
    for k in range(2):
        came(k, 3, 3, 0)
        came(k, 3, 3, 1)
    query_blocks(1, lambda t: (3, 3))
    for group in ((4, 5), (1, 3, 7)):
        for o in group:
            if o in (4, 5):
                share_msg(o).wait_recv()
            else:
                pool_msg[o].wait_recv()
        kv_blocks(tuple(peer_from(o) for o in group))

    def span(n, carry):
        rows = pl.ds(pl.multiple_of(n * SPAN, SPAN), SPAN)
        mean = jnp.sum(ssq[rows, :], axis=1, keepdims=True) * (1.0 / D)
        scale = lax.rsqrt(mean + 1e-05) * DH**-0.5
        j0, j1 = place_s[2 * n], place_s[2 * n + 1]
        for h in range(4):
            cols = slice(h * DH, (h + 1) * DH)
            q = (acc[rows, cols] * scale).astype(BF16)
            s0, s1 = _dot(q, keys[j0, cols, :]), _dot(q, keys[j1, cols, :])
            top = jnp.max(jnp.maximum(s0, s1), axis=1, keepdims=True)
            e0, e1 = jnp.exp(s0 - top), jnp.exp(s1 - top)
            weigh = 1.0 / jnp.sum(e0 + e1, axis=1, keepdims=True)
            o = _dot(e0.astype(BF16), values[j0, :, cols]) + _dot(e1.astype(BF16), values[j1, :, cols])
            att[rows, cols] = (o * weigh).astype(BF16)
        return carry

    loads[4].wait()

    def block(k, a, b):
        s = column(k, a, b)
        return _dot(
            att[pl.ds(pl.multiple_of(k * HALF, HALF), HALF), :],
            wo[:, pl.ds(pl.multiple_of(s * HC, HC), HC)],
        )

    def one_h(k, i, h):
        return pltpu.make_async_remote_copy(
            send1.at[k, i, 0, pl.ds(h * QUART, QUART)], recv1h.at[k, i, h],
            rs1h_send.at[k, i, h], rs1h_recv.at[k, i, h],
            device_id=along(k, 2, 1 if h == 0 else -1), device_id_type=MESH,
        )

    def one(k, i, d):
        return pltpu.make_async_remote_copy(
            send1.at[k, i, 1 + d], recv1.at[k, i, d], rs1_send.at[k, i, d], rs1_recv.at[k, i, d],
            device_id=along(k, 2, 1 if d == 0 else -1), device_id_type=MESH,
        )

    def two_h(k, h):
        return pltpu.make_async_remote_copy(
            send2.at[k, 0, pl.ds(h * QUART, QUART)], recv2h.at[k, h],
            rs2_send.at[k, h], rs2_recv.at[k, h],
            device_id=along(k, 1, 1 if h == 0 else -1), device_id_type=MESH,
        )

    def two(k, d):
        return pltpu.make_async_remote_copy(
            send2.at[k, 1 + d], recv2.at[k, d], rs2_send.at[k, 2 + d], rs2_recv.at[k, 2 + d],
            device_id=along(k, 1, 1 if d == 0 else -1), device_id_type=MESH,
        )

    FAR = (3, 1, 2, 0)
    for k in range(2):
        lax.fori_loop(4 * k, 4 * k + 4, span, 0, unroll=4)
        for i in FAR:
            send1[k, i, 0] = block(k, STEP[i], 2).astype(BF16)
            for h in range(2):
                one_h(k, i, h).start()
    for i in FAR:
        for k in range(2):
            for d in range(2):
                one_h(k, i, d).wait_recv()
                part = block(k, STEP[i], 1 if d == 0 else -1)
                at = pl.ds(d * QUART, QUART)
                rest = pl.ds((1 - d) * QUART, QUART)
                got = recv1h[k, i, d].astype(F32)
                send1[k, i, 1 + d, at] = (part[d * QUART : (d + 1) * QUART] + got).astype(BF16)
                send1[k, i, 1 + d, rest] = part[(1 - d) * QUART : (2 - d) * QUART].astype(BF16)
                one(k, i, d).start()
    for i in FAR:
        for k in range(2):
            for d in range(2):
                one(k, i, d).wait_recv()
            total = block(k, STEP[i], 0) + recv1[k, i, 0].astype(F32) + recv1[k, i, 1].astype(F32)
            if i == 3:
                send2[k, 0] = total.astype(BF16)
                for h in range(2):
                    two_h(k, h).start()
            elif i:
                d = i - 1
                two_h(k, d).wait_recv()
                at = pl.ds(d * QUART, QUART)
                rest = pl.ds((1 - d) * QUART, QUART)
                got = recv2h[k, d].astype(F32)
                send2[k, 1 + d, at] = (total[d * QUART : (d + 1) * QUART] + got).astype(BF16)
                send2[k, 1 + d, rest] = total[(1 - d) * QUART : (2 - d) * QUART].astype(BF16)
                two(k, d).start()
            else:
                for d in range(2):
                    two(k, d).wait_recv()
                total = total + recv2[k, 0].astype(F32) + recv2[k, 1].astype(F32)
                own = slots[k, 0, 0].astype(F32)
                out_ref[pl.ds(k * HALF, HALF), :] = (own + total).astype(BF16)

    for msg in started:
        msg.wait_send()
    for msg in kv_msg:
        msg.wait_send()
    for o in ORDER:
        req_msg[o].wait_send()
        pool_msg[o].wait_send()
        wy_msg[o].wait_send()
    for o in (4, 5):
        share_msg(o).wait_send()
    for k in range(2):
        for i in range(4):
            for d in range(2):
                one_h(k, i, d).wait_send()
                one(k, i, d).wait_send()
        for d in range(2):
            two_h(k, d).wait_send()
            two(k, d).wait_send()


def on_device(
    tokens, norm_gain, query_weight, kv_weight, out_weight, neighbour_pool, neighbour_shard, neighbour_slot
):
    gain = norm_gain.reshape(16, 4, 128)
    vmem, hbm = pl.BlockSpec(memory_space=pltpu.VMEM), pl.BlockSpec(memory_space=pl.ANY)
    dma = pltpu.SemaphoreType.DMA
    return pl.pallas_call(
        kernel,
        out_shape=jax.ShapeDtypeStruct((ROWS, HC), BF16),
        in_specs=[hbm, vmem, vmem, vmem, hbm, hbm, hbm, hbm],
        out_specs=vmem,
        scratch_shapes=[
            pltpu.VMEM((2, 4, 4, HALF, HC), BF16),
            pltpu.VMEM((D, HC), BF16),
            pltpu.VMEM((ROWS, HC), F32),
            pltpu.VMEM((ROWS, 128), F32),
            pltpu.VMEM((16, NL, ENC), BF16),
            pltpu.VMEM((16, NL, ENC), BF16),
            pltpu.VMEM((16, NL, ENC), BF16),
            pltpu.VMEM((16, HC, NL), BF16),
            pltpu.VMEM((16, NL, HC), BF16),
            pltpu.VMEM((16, EROWS, 2, DH), BF16),
            pltpu.VMEM((16, EPAD, DH), BF16),
            pltpu.VMEM((16, EPAD, DH), BF16),
            pltpu.VMEM((ENC, DH), F32),
            pltpu.VMEM((2, ENC, HC), BF16),
            pltpu.VMEM((8, 128), I32),
            pltpu.VMEM((8, 8, 128), I32),
            pltpu.SMEM((8, 8, 128), I32),
            pltpu.SMEM((16,), I32),
            pltpu.VMEM((ROWS, HC), BF16),
            pltpu.VMEM((HC, D), BF16),
            pltpu.VMEM((2, 4, 3, HALF, HC), BF16),
            pltpu.VMEM((2, 4, 2, QUART, HC), BF16),
            pltpu.VMEM((2, 4, 2, HALF, HC), BF16),
            pltpu.VMEM((2, 3, HALF, HC), BF16),
            pltpu.VMEM((2, 2, QUART, HC), BF16),
            pltpu.VMEM((2, 2, HALF, HC), BF16),
            dma((6,)), dma((16,)), dma((2, 4, 4, 2)), dma((2, 4, 4, 2)), dma((8,)), dma((8,)),
            dma((16,)), dma((16,)), dma((8,)), dma((8,)), dma((8,)), dma((8,)), dma((2,)), dma((2,)),
            dma((2, 4, 2)), dma((2, 4, 2)), dma((2, 4, 2)), dma((2, 4, 2)), dma((2, 4)), dma((2, 4)),
        ],
        compiler_params=pltpu.CompilerParams(
            collective_id=0, has_side_effects=True, vmem_limit_bytes=62 << 20
        ),
        cost_estimate=pl.CostEstimate(
            flops=13_000_000_000, bytes_accessed=24_000_000, transcendentals=600_000
        ),
        name="retro_block",
    )(tokens, gain, neighbour_shard.T, neighbour_slot.T, query_weight, kv_weight, out_weight, neighbour_pool)


def solution(mesh):
    return jax.shard_map(
        on_device,
        mesh=mesh,
        in_specs=(
            P("retr", "store"),
            P(),
            P(None, "store"),
            P("store", None, None),
            P("store", None),
            P("retr", None, None),
            P("retr", None),
            P("retr", None),
        ),
        out_specs=P("retr", "store"),
        check_vma=False,
    )
```

```python
import jax
import jax.numpy as jnp
from jax import lax
from jax.experimental import pallas as pl
from jax.experimental.pallas import tpu as pltpu
from jax.sharding import PartitionSpec as P

MESH = pl.DeviceIdType.MESH
BF16, F32, I32 = jnp.bfloat16, jnp.float32, jnp.int32

DH, ENC, SPAN, NL, NEIGH = 128, 896, 64, 128, 2
D, HC, ROWS, HALF, QUART = 8192, 512, 512, 256, 128
EROWS, EPAD = 56, 64
STEP = (0, 1, -1, 2)


def _dot(a, b):
    return jnp.dot(a, b, preferred_element_type=F32)


def kernel(
    tok_ref, gain_hbm, shard_hbm, slot_hbm, wq_hbm, kvw_hbm, wo_hbm, pool_hbm, out_ref,
    slots, wq, acc, ssq, pool, picked, fetched, keys, values, kvraw, kvsend, kvrecv, w32, wkv,
    reqs, table, table_s, place_s, att, wo, send1, recv1h, recv1, send2, recv2h, recv2,
    gain_ref, shard_ref, slot_ref, load_sem, raw_sem, ag_send, ag_recv, req_send, req_recv, kv_send, kv_recv,
    wy_send, wy_recv, pool_send, pool_recv, share_send, share_recv, rs1h_send, rs1h_recv, rs1_send, rs1_recv,
    rs2_send, rs2_recv,
):
    retr, store = lax.axis_index("retr"), lax.axis_index("store")
    x, z = store // 4, store % 4
    y, c = retr // 2, retr % 2

    def device(dx, dy, dz, dc):
        return ((y + dy + 4) % 4 * 2 + (c + dc) % 2, (x + dx + 4) % 4 * 4 + (z + dz + 4) % 4)

    def along(kind, axis, step):
        return device(step, 0, 0, 0) if (kind == 0) == (axis == 1) else device(0, 0, step, 0)

    def column(kind, a, b):
        dx = jnp.where(kind == 0, a, b)
        dz = jnp.where(kind == 0, b, a)
        return (x + dx + 4) % 4 * 4 + (z + dz + 4) % 4

    def offset(i):
        return jnp.where(i == 0, 0, jnp.where(i == 1, 1, jnp.where(i == 2, -1, 2)))

    loads = [
        pltpu.make_async_copy(tok_ref.at[pl.ds(0, HALF)], slots.at[0, 0, 0], load_sem.at[0]),
        pltpu.make_async_copy(tok_ref.at[pl.ds(HALF, HALF)], slots.at[1, 0, 0], load_sem.at[1]),
        pltpu.make_async_copy(pool_hbm, pool, load_sem.at[2]),
        pltpu.make_async_copy(wq_hbm, wq, load_sem.at[3]),
        pltpu.make_async_copy(wo_hbm, wo, load_sem.at[4]),
    ]
    small = [
        pltpu.make_async_copy(shard_hbm, shard_ref, load_sem.at[6]),
        pltpu.make_async_copy(slot_hbm, slot_ref, load_sem.at[7]),
        pltpu.make_async_copy(gain_hbm, gain_ref, load_sem.at[8]),
    ]
    for copy in [*small, loads[0], loads[1]]:
        copy.start()
    raws = [
        pltpu.make_async_copy(
            kvw_hbm.at[:, :, pl.ds(s * HC + y * DH, DH)], kvraw.at[s], raw_sem.at[s]
        )
        for s in range(16)
    ]
    for copy in raws:
        copy.start()
    for copy in loads[2:]:
        copy.start()

    barrier = pltpu.get_barrier_semaphore()
    peers = [(dx, 0, dz, 0) for dx in STEP for dz in STEP if dx or dz]
    peers += [(0, dy, 0, dc) for dy in STEP for dc in (0, 1) if dy or dc]
    for peer in sorted(peers, key=lambda p: -sum(map(abs, p))):
        pl.semaphore_signal(barrier, inc=1, device_id=device(*peer), device_id_type=MESH)
    reqs[...] = jnp.zeros((8, 128), I32)
    for copy in small:
        copy.wait()
    reqs[0:2, 0:8] = shard_ref[...]
    reqs[2:4, 0:8] = slot_ref[...]

    pl.semaphore_wait(barrier, 22)

    RET = [(o // 2, o % 2) for o in range(8)]
    EARLY, LATE = [4, 5, 2, 6], [3, 7, 1]
    ORDER = EARLY + LATE

    def peer_from(o):
        dy, dc = RET[o]
        return (y - dy + 4) % 4 * 2 + (c + dc) % 2

    req_msg = {}
    for o in ORDER:
        req_msg[o] = pltpu.make_async_remote_copy(
            reqs, table.at[retr], req_send.at[o], req_recv.at[o],
            device_id=device(0, RET[o][0], 0, RET[o][1]), device_id_type=MESH,
        )
        req_msg[o].start()

    def gather_msg(k, i, j, h):
        axis = 2 if j else 1
        move = j if j else i
        if move == 3:
            src_move, step, half = (1, -1, 0) if h == 0 else (2, 1, 1)
            src = (i, src_move) if j else (src_move, 0)
            rows = pl.ds(half * QUART, QUART)
            return pltpu.make_async_remote_copy(
                slots.at[k, src[0], src[1], rows], slots.at[k, i, j, rows],
                ag_send.at[k, i, j, h], ag_recv.at[k, i, j, h],
                device_id=along(k, axis, step), device_id_type=MESH,
            )
        src = (i, 0) if j else (0, 0)
        step = -1 if move == 1 else 1
        return pltpu.make_async_remote_copy(
            slots.at[k, src[0], src[1]], slots.at[k, i, j],
            ag_send.at[k, i, j, 0], ag_recv.at[k, i, j, 0],
            device_id=along(k, axis, step), device_id_type=MESH,
        )

    started = []

    def go(k, i, j, h=0):
        msg = gather_msg(k, i, j, h)
        msg.start()
        started.append(msg)

    def came(k, i, j, h=0):
        gather_msg(k, i, j, h).wait_recv()

    loads[0].wait()
    loads[1].wait()
    for k in range(2):
        go(k, 1, 0)
        go(k, 2, 0)
    for k in range(2):
        go(k, 0, 1)
        go(k, 0, 2)

    for copy in raws:
        copy.wait()

    def split(s, carry):
        raw = kvraw[s].astype(F32)
        one = jnp.where(c == 0, raw[:, 0, :], raw[:, 1, :])
        kvsend[s] = jnp.concatenate([one, jnp.zeros((EPAD - EROWS, DH), F32)], axis=0).astype(BF16)
        return carry

    lax.fori_loop(0, 16, split, 0)
    kv_msg = []
    for o in range(1, 16):
        to = (store + o) % 16
        msg = pltpu.make_async_remote_copy(
            kvsend.at[to], kvrecv.at[store], kv_send.at[o], kv_recv.at[o],
            device_id=(retr, to), device_id_type=MESH,
        )
        msg.start()
        kv_msg.append(msg)
    kvrecv[store] = kvsend[store]

    acc[...] = jnp.zeros((ROWS, HC), F32)
    ssq[...] = jnp.zeros((ROWS, 128), F32)

    def query_block(k, i, j):
        s = column(k, offset(i), offset(j))
        rows = pl.ds(k * HALF, HALF)
        xf = slots[k, i, j].astype(F32)
        sq = xf * xf
        ssq[rows, :] += (sq[:, 0:128] + sq[:, 128:256]) + (sq[:, 256:384] + sq[:, 384:512])
        g4 = gain_ref[s]
        g = jnp.concatenate([g4[t : t + 1, :] for t in range(4)], axis=1)
        acc[rows, :] += _dot((xf * g).astype(BF16), wq[pl.ds(pl.multiple_of(s * HC, HC), HC), :])

    def query_blocks(n, place):
        def body(t, carry):
            i, j = place(t // 2)
            query_block(t % 2, i, j)
            return carry

        lax.fori_loop(0, 2 * n, body, 0)

    table[retr] = reqs[...]
    for o in ORDER:
        req_msg[o].wait_recv()
    to_smem = pltpu.make_async_copy(table, table_s, load_sem.at[5])
    to_smem.start()
    to_smem.wait()
    loads[2].wait()
    def parity(o):
        return (x if o == 4 else z) % 2

    def share_msg(o):
        at = pl.ds(2 * peer_from(o) + parity(o), 1)
        step = 1 - 2 * ((parity(o) + c) % 2)
        return pltpu.make_async_remote_copy(
            fetched.at[at], fetched.at[at], share_send.at[o - 4], share_recv.at[o - 4],
            device_id=device(step, 0, 0, 0) if o == 4 else device(0, 0, step, 0),
            device_id_type=MESH,
        )

    pool_msg = {}
    for o in [*ORDER, 0]:
        dy, dc = RET[o]
        to = (y + dy) % 4 * 2 + (c + dc) % 2
        first, second, seen = I32(0), I32(0), I32(0)
        for n in range(16):
            hit = table_s[to, n % 2, n // 2] == retr
            slot = table_s[to, 2 + n % 2, n // 2]
            first = jnp.where(hit & (seen == 0), slot, first)
            second = jnp.where(hit & (seen == 1), slot, second)
            seen = seen + jnp.where(hit, 1, 0)
        if o == 0:
            fetched[2 * retr] = pool[first]
            fetched[2 * retr + 1] = pool[second]
            continue
        picked[2 * o] = pool[first]
        picked[2 * o + 1] = pool[second]
        n, skip = (1, parity(o)) if dy == 2 else (2, 0)
        pool_msg[o] = pltpu.make_async_remote_copy(
            picked.at[pl.ds(2 * o + skip, n)], fetched.at[pl.ds(2 * retr + skip, n)],
            pool_send.at[o], pool_recv.at[o],
            device_id=device(0, dy, 0, dc), device_id_type=MESH,
        )
        if o in EARLY:
            pool_msg[o].start()
    mine = [table_s[retr, n % 2, n // 2] for n in range(16)]
    for n in range(16):
        before = I32(0)
        for m in range(n):
            before = before + jnp.where(mine[m] == mine[n], 1, 0)
        place_s[n] = 2 * mine[n] + before

    loads[3].wait()
    query_blocks(1, lambda t: (0, 0))

    for k in range(2):
        came(k, 1, 0)
        go(k, 3, 0, 0)
        go(k, 1, 1)
        go(k, 1, 2)
        came(k, 2, 0)
        go(k, 3, 0, 1)
        go(k, 2, 1)
        go(k, 2, 2)
    query_blocks(2, lambda t: (1 + t, 0))

    for msg in kv_msg:
        msg.wait_recv()

    def assemble(s, carry):
        part = kvrecv[s].astype(F32)
        w32[pl.ds(pl.multiple_of(s * EROWS, 8), EROWS), :] = part[:EROWS]
        return carry

    lax.fori_loop(0, 16, assemble, 0)
    wkv[c, :, pl.ds(pl.multiple_of(y * DH, DH), DH)] = w32[...].astype(BF16)

    def weight_part(dy, dc):
        return wkv.at[(c + dc) % 2, :, pl.ds(pl.multiple_of((y - dy + 4) % 4 * DH, DH), DH)]

    def weight_msg(o):
        dy, dc = RET[o]
        if dc:
            return pltpu.make_async_remote_copy(
                weight_part(dy, 0), weight_part(dy, 0), wy_send.at[o], wy_recv.at[o],
                device_id=device(0, 0, 0, 1), device_id_type=MESH,
            )
        return pltpu.make_async_remote_copy(
            weight_part(0, 0), weight_part(0, 0), wy_send.at[o], wy_recv.at[o],
            device_id=device(0, dy, 0, 0), device_id_type=MESH,
        )

    wy_msg = {}

    def weight_go(o):
        wy_msg[o] = weight_msg(o)
        wy_msg[o].start()

    for o in (2, 6, 4, 1):
        weight_go(o)
    for o in LATE:
        pool_msg[o].start()

    for k in range(2):
        came(k, 0, 1)
        go(k, 0, 3, 0)
        came(k, 0, 2)
        go(k, 0, 3, 1)
    query_blocks(2, lambda t: (0, 1 + t))
    for k in range(2):
        came(k, 3, 0, 0)
        came(k, 3, 0, 1)
        go(k, 3, 1)
        go(k, 3, 2)
    query_blocks(1, lambda t: (3, 0))
    for i in (1, 2):
        for k in range(2):
            came(k, i, 1)
            go(k, i, 3, 0)
            came(k, i, 2)
            go(k, i, 3, 1)
    query_blocks(4, lambda t: (1 + t // 2, 1 + t % 2))

    for o in (4, 5):
        pool_msg[o].wait_recv()
        share_msg(o).start()
    for k in range(2):
        came(k, 3, 1)
        go(k, 3, 3, 0)
        came(k, 3, 2)
        go(k, 3, 3, 1)
    query_blocks(2, lambda t: (3, 1 + t))
    for o in (2, 6, 4):
        wy_msg[o].wait_recv()
        weight_go(o + 1)

    def kv_block(r):
        ctx = fetched[pl.ds(2 * r, 2)].reshape(2 * NL, ENC)
        turned = _dot(ctx, wkv[0]).astype(BF16).T
        keys[2 * r] = turned[:, :NL]
        keys[2 * r + 1] = turned[:, NL:]
        values[pl.ds(2 * r, 2)] = _dot(ctx, wkv[1]).astype(BF16).reshape(2, NL, HC)


    def kv_blocks(sources):
        def body(t, carry):
            r = sources[0]
            for n in range(1, len(sources)):
                r = jnp.where(t == n, sources[n], r)
            kv_block(r)
            return carry

        lax.fori_loop(0, len(sources), body, 0)

    for o in (1, 3, 5, 7):
        wy_msg[o].wait_recv()
    for o in (1, 2, 6):
        pool_msg[o].wait_recv()
    kv_blocks((retr, *(peer_from(o) for o in (1, 2, 6))))
    for k in range(2):
        for i in range(3):
            came(k, i, 3, 0)
            came(k, i, 3, 1)
    query_blocks(3, lambda t: (t, 3))
    for o in (4, 5):
        share_msg(o).wait_recv()
    kv_blocks((peer_from(4), peer_from(5)))
    for o in (3, 7):
        pool_msg[o].wait_recv()
    kv_blocks((peer_from(3), peer_from(7)))

    def span(n, carry):
        rows = pl.ds(pl.multiple_of(n * SPAN, SPAN), SPAN)
        mean = jnp.sum(ssq[rows, :], axis=1, keepdims=True) * (1.0 / D)
        scale = lax.rsqrt(mean + 1e-05) * DH**-0.5
        j0, j1 = place_s[2 * n], place_s[2 * n + 1]
        for h in range(4):
            cols = slice(h * DH, (h + 1) * DH)
            q = (acc[rows, cols] * scale).astype(BF16)
            s0, s1 = _dot(q, keys[j0, cols, :]), _dot(q, keys[j1, cols, :])
            top = jnp.max(jnp.maximum(s0, s1), axis=1, keepdims=True)
            e0, e1 = jnp.exp(s0 - top), jnp.exp(s1 - top)
            weigh = 1.0 / jnp.sum(e0 + e1, axis=1, keepdims=True)
            o = _dot(e0.astype(BF16), values[j0, :, cols]) + _dot(e1.astype(BF16), values[j1, :, cols])
            att[rows, cols] = (o * weigh).astype(BF16)
        return carry

    loads[4].wait()

    def block(k, a, b):
        s = column(k, a, b)
        return _dot(
            att[pl.ds(pl.multiple_of(k * HALF, HALF), HALF), :],
            wo[:, pl.ds(pl.multiple_of(s * HC, HC), HC)],
        )

    def one_h(k, i, h):
        return pltpu.make_async_remote_copy(
            send1.at[k, i, 0, pl.ds(h * QUART, QUART)], recv1h.at[k, i, h],
            rs1h_send.at[k, i, h], rs1h_recv.at[k, i, h],
            device_id=along(k, 2, 1 if h == 0 else -1), device_id_type=MESH,
        )

    def one(k, i, d):
        return pltpu.make_async_remote_copy(
            send1.at[k, i, 1 + d], recv1.at[k, i, d], rs1_send.at[k, i, d], rs1_recv.at[k, i, d],
            device_id=along(k, 2, 1 if d == 0 else -1), device_id_type=MESH,
        )

    def two_h(k, h):
        return pltpu.make_async_remote_copy(
            send2.at[k, 0, pl.ds(h * QUART, QUART)], recv2h.at[k, h],
            rs2_send.at[k, h], rs2_recv.at[k, h],
            device_id=along(k, 1, 1 if h == 0 else -1), device_id_type=MESH,
        )

    def two(k, d):
        return pltpu.make_async_remote_copy(
            send2.at[k, 1 + d], recv2.at[k, d], rs2_send.at[k, 2 + d], rs2_recv.at[k, 2 + d],
            device_id=along(k, 1, 1 if d == 0 else -1), device_id_type=MESH,
        )

    FAR = (3, 1, 2, 0)
    def far(k, i):
        send1[k, i, 0] = block(k, STEP[i], 2).astype(BF16)
        for h in range(2):
            one_h(k, i, h).start()

    for k in range(2):
        came(k, 3, 3, 0)
        came(k, 3, 3, 1)
        query_block(k, 3, 3)
        lax.fori_loop(4 * k, 4 * k + 4, span, 0, unroll=4)
        for i in (3, 1):
            far(k, i)
    def to_neighbours(i):
        for k in range(2):
            for d in range(2):
                one_h(k, i, d).wait_recv()
                part = block(k, STEP[i], 1 if d == 0 else -1)
                at = pl.ds(d * QUART, QUART)
                rest = pl.ds((1 - d) * QUART, QUART)
                got = recv1h[k, i, d].astype(F32)
                send1[k, i, 1 + d, at] = (part[d * QUART : (d + 1) * QUART] + got).astype(BF16)
                send1[k, i, 1 + d, rest] = part[(1 - d) * QUART : (2 - d) * QUART].astype(BF16)
                one(k, i, d).start()
    def across(i):
        for k in range(2):
            for d in range(2):
                one(k, i, d).wait_recv()
            total = block(k, STEP[i], 0) + recv1[k, i, 0].astype(F32) + recv1[k, i, 1].astype(F32)
            if i == 3:
                send2[k, 0] = total.astype(BF16)
                for h in range(2):
                    two_h(k, h).start()
            elif i:
                d = i - 1
                two_h(k, d).wait_recv()
                at = pl.ds(d * QUART, QUART)
                rest = pl.ds((1 - d) * QUART, QUART)
                got = recv2h[k, d].astype(F32)
                send2[k, 1 + d, at] = (total[d * QUART : (d + 1) * QUART] + got).astype(BF16)
                send2[k, 1 + d, rest] = total[(1 - d) * QUART : (2 - d) * QUART].astype(BF16)
                two(k, d).start()
            else:
                for d in range(2):
                    two(k, d).wait_recv()
                total = total + recv2[k, 0].astype(F32) + recv2[k, 1].astype(F32)
                own = slots[k, 0, 0].astype(F32)
                out_ref[pl.ds(k * HALF, HALF), :] = (own + total).astype(BF16)

    to_neighbours(3)
    for k in range(2):
        far(k, 2)
    to_neighbours(1)
    across(3)
    for k in range(2):
        far(k, 0)
    to_neighbours(2)
    across(1)
    to_neighbours(0)
    across(2)
    across(0)

    for msg in started:
        msg.wait_send()
    for msg in kv_msg:
        msg.wait_send()
    for o in ORDER:
        req_msg[o].wait_send()
        pool_msg[o].wait_send()
        wy_msg[o].wait_send()
    for o in (4, 5):
        share_msg(o).wait_send()
    for k in range(2):
        for i in range(4):
            for d in range(2):
                one_h(k, i, d).wait_send()
                one(k, i, d).wait_send()
        for d in range(2):
            two_h(k, d).wait_send()
            two(k, d).wait_send()


def on_device(
    tokens, norm_gain, query_weight, kv_weight, out_weight, neighbour_pool, neighbour_shard, neighbour_slot
):
    gain = norm_gain.reshape(16, 4, 128)
    vmem, hbm = pl.BlockSpec(memory_space=pltpu.VMEM), pl.BlockSpec(memory_space=pl.ANY)
    dma = pltpu.SemaphoreType.DMA
    return pl.pallas_call(
        kernel,
        out_shape=jax.ShapeDtypeStruct((ROWS, HC), BF16),
        in_specs=[hbm] * 8,
        out_specs=vmem,
        scratch_shapes=[
            pltpu.VMEM((2, 4, 4, HALF, HC), BF16),
            pltpu.VMEM((D, HC), BF16),
            pltpu.VMEM((ROWS, HC), F32),
            pltpu.VMEM((ROWS, 128), F32),
            pltpu.VMEM((16, NL, ENC), BF16),
            pltpu.VMEM((16, NL, ENC), BF16),
            pltpu.VMEM((16, NL, ENC), BF16),
            pltpu.VMEM((16, HC, NL), BF16),
            pltpu.VMEM((16, NL, HC), BF16),
            pltpu.VMEM((16, EROWS, 2, DH), BF16),
            pltpu.VMEM((16, EPAD, DH), BF16),
            pltpu.VMEM((16, EPAD, DH), BF16),
            pltpu.VMEM((ENC, DH), F32),
            pltpu.VMEM((2, ENC, HC), BF16),
            pltpu.VMEM((8, 128), I32),
            pltpu.VMEM((8, 8, 128), I32),
            pltpu.SMEM((8, 8, 128), I32),
            pltpu.SMEM((16,), I32),
            pltpu.VMEM((ROWS, HC), BF16),
            pltpu.VMEM((HC, D), BF16),
            pltpu.VMEM((2, 4, 3, HALF, HC), BF16),
            pltpu.VMEM((2, 4, 2, QUART, HC), BF16),
            pltpu.VMEM((2, 4, 2, HALF, HC), BF16),
            pltpu.VMEM((2, 3, HALF, HC), BF16),
            pltpu.VMEM((2, 2, QUART, HC), BF16),
            pltpu.VMEM((2, 2, HALF, HC), BF16),
            pltpu.VMEM((16, 4, 128), F32),
            pltpu.VMEM((2, 8), I32),
            pltpu.VMEM((2, 8), I32),
            dma((9,)), dma((16,)), dma((2, 4, 4, 2)), dma((2, 4, 4, 2)), dma((8,)), dma((8,)),
            dma((16,)), dma((16,)), dma((8,)), dma((8,)), dma((8,)), dma((8,)), dma((2,)), dma((2,)),
            dma((2, 4, 2)), dma((2, 4, 2)), dma((2, 4, 2)), dma((2, 4, 2)), dma((2, 4)), dma((2, 4)),
        ],
        compiler_params=pltpu.CompilerParams(
            collective_id=0, has_side_effects=True, vmem_limit_bytes=62 << 20
        ),
        cost_estimate=pl.CostEstimate(
            flops=13_000_000_000, bytes_accessed=24_000_000, transcendentals=600_000
        ),
        name="retro_block",
    )(tokens, gain, neighbour_shard.T, neighbour_slot.T, query_weight, kv_weight, out_weight, neighbour_pool)


def solution(mesh):
    return jax.shard_map(
        on_device,
        mesh=mesh,
        in_specs=(
            P("retr", "store"),
            P(),
            P(None, "store"),
            P("store", None, None),
            P("store", None),
            P("retr", None, None),
            P("retr", None),
            P("retr", None),
        ),
        out_specs=P("retr", "store"),
        check_vma=False,
    )
```

```python
import jax
import jax.numpy as jnp
from jax import lax
from jax.experimental import pallas as pl
from jax.experimental.pallas import tpu as pltpu
from jax.sharding import PartitionSpec as P

MESH = pl.DeviceIdType.MESH
BF16, F32, I32 = jnp.bfloat16, jnp.float32, jnp.int32

DH, ENC, SPAN, NL, NEIGH = 128, 896, 64, 128, 2
D, HC, ROWS, HALF, QUART = 8192, 512, 512, 256, 128
EROWS, EPAD = 56, 64
STEP = (0, 1, -1, 2)


def _dot(a, b):
    return jnp.dot(a, b, preferred_element_type=F32)


def kernel(
    tok_ref, gain_hbm, shard_hbm, slot_hbm, wq_hbm, kvw_hbm, wo_hbm, pool_hbm, out_ref,
    slots, wq, acc, ssq, pool, picked, fetched, keys, values, kvraw, kvsend, kvrecv, w32, wkv,
    reqs, table, table_s, place_s, att, wo, send1, recv1h, recv1, send2, recv2h, recv2,
    gain_ref, shard_ref, slot_ref, load_sem, raw_sem, ag_send, ag_recv, req_send, req_recv, kv_send, kv_recv,
    wy_send, wy_recv, pool_send, pool_recv, share_send, share_recv, won_send, won_recv, rs1h_send, rs1h_recv, rs1_send, rs1_recv,
    rs2_send, rs2_recv,
):
    retr, store = lax.axis_index("retr"), lax.axis_index("store")
    x, z = store // 4, store % 4
    y, c = retr // 2, retr % 2

    def device(dx, dy, dz, dc):
        return ((y + dy + 4) % 4 * 2 + (c + dc) % 2, (x + dx + 4) % 4 * 4 + (z + dz + 4) % 4)

    def along(kind, axis, step):
        return device(step, 0, 0, 0) if (kind == 0) == (axis == 1) else device(0, 0, step, 0)

    def column(kind, a, b):
        dx = jnp.where(kind == 0, a, b)
        dz = jnp.where(kind == 0, b, a)
        return (x + dx + 4) % 4 * 4 + (z + dz + 4) % 4

    def offset(i):
        return jnp.where(i == 0, 0, jnp.where(i == 1, 1, jnp.where(i == 2, -1, 2)))

    loads = [
        pltpu.make_async_copy(tok_ref.at[pl.ds(0, HALF)], slots.at[0, 0, 0], load_sem.at[0]),
        pltpu.make_async_copy(tok_ref.at[pl.ds(HALF, HALF)], slots.at[1, 0, 0], load_sem.at[1]),
        pltpu.make_async_copy(pool_hbm, pool, load_sem.at[2]),
        pltpu.make_async_copy(wq_hbm, wq, load_sem.at[3]),
        pltpu.make_async_copy(wo_hbm, wo, load_sem.at[4]),
    ]
    small = [
        pltpu.make_async_copy(shard_hbm, shard_ref, load_sem.at[6]),
        pltpu.make_async_copy(slot_hbm, slot_ref, load_sem.at[7]),
        pltpu.make_async_copy(gain_hbm, gain_ref, load_sem.at[8]),
    ]
    for copy in [*small, loads[0], loads[1]]:
        copy.start()
    barrier = pltpu.get_barrier_semaphore()
    peers = [(dx, 0, dz, 0) for dx in STEP for dz in STEP if dx or dz]
    peers += [(0, dy, 0, dc) for dy in STEP for dc in (0, 1) if dy or dc]
    for peer in sorted(peers, key=lambda p: -sum(map(abs, p))):
        pl.semaphore_signal(barrier, inc=1, device_id=device(*peer), device_id_type=MESH)
    raws = [
        pltpu.make_async_copy(
            kvw_hbm.at[:, :, pl.ds(s * HC + y * DH, DH)], kvraw.at[s], raw_sem.at[s]
        )
        for s in range(16)
    ]
    for copy in raws:
        copy.start()
    for copy in loads[2:]:
        copy.start()
    reqs[...] = jnp.zeros((8, 128), I32)
    for copy in small:
        copy.wait()
    reqs[0:2, 0:8] = shard_ref[...]
    reqs[2:4, 0:8] = slot_ref[...]

    pl.semaphore_wait(barrier, 22)

    RET = [(o // 2, o % 2) for o in range(8)]
    EARLY, LATE, LAST = [4, 5], [2, 6, 1], [3, 7]
    ORDER = EARLY + LATE + LAST

    def peer_from(o):
        dy, dc = RET[o]
        return (y - dy + 4) % 4 * 2 + (c + dc) % 2

    def gather_msg(k, i, j, h):
        axis = 2 if j else 1
        move = j if j else i
        if move == 3:
            src_move, step, half = (1, -1, 0) if h == 0 else (2, 1, 1)
            src = (i, src_move) if j else (src_move, 0)
            rows = pl.ds(half * QUART, QUART)
            return pltpu.make_async_remote_copy(
                slots.at[k, src[0], src[1], rows], slots.at[k, i, j, rows],
                ag_send.at[k, i, j, h], ag_recv.at[k, i, j, h],
                device_id=along(k, axis, step), device_id_type=MESH,
            )
        src = (i, 0) if j else (0, 0)
        step = -1 if move == 1 else 1
        return pltpu.make_async_remote_copy(
            slots.at[k, src[0], src[1]], slots.at[k, i, j],
            ag_send.at[k, i, j, 0], ag_recv.at[k, i, j, 0],
            device_id=along(k, axis, step), device_id_type=MESH,
        )

    started = []

    def go(k, i, j, h=0):
        msg = gather_msg(k, i, j, h)
        msg.start()
        started.append(msg)

    def came(k, i, j, h=0):
        gather_msg(k, i, j, h).wait_recv()

    loads[0].wait()
    loads[1].wait()
    for k in range(2):
        go(k, 1, 0)
        go(k, 2, 0)
    req_msg = {}
    for o in ORDER:
        req_msg[o] = pltpu.make_async_remote_copy(
            reqs, table.at[retr], req_send.at[o], req_recv.at[o],
            device_id=device(0, RET[o][0], 0, RET[o][1]), device_id_type=MESH,
        )
        req_msg[o].start()
    for k in range(2):
        go(k, 0, 1)
        go(k, 0, 2)

    for copy in raws:
        copy.wait()

    def split(s, carry):
        raw = kvraw[s].astype(F32)
        one = jnp.where(c == 0, raw[:, 0, :], raw[:, 1, :])
        kvsend[s] = jnp.concatenate([one, jnp.zeros((EPAD - EROWS, DH), F32)], axis=0).astype(BF16)
        return carry

    lax.fori_loop(0, 16, split, 0)
    kv_msg = []
    for o in range(1, 16):
        to = (store + o) % 16
        msg = pltpu.make_async_remote_copy(
            kvsend.at[to], kvrecv.at[store], kv_send.at[o], kv_recv.at[o],
            device_id=(retr, to), device_id_type=MESH,
        )
        msg.start()
        kv_msg.append(msg)
    kvrecv[store] = kvsend[store]

    acc[...] = jnp.zeros((ROWS, HC), F32)
    ssq[...] = jnp.zeros((ROWS, 128), F32)

    def query_block(k, i, j):
        s = column(k, offset(i), offset(j))
        rows = pl.ds(k * HALF, HALF)
        xf = slots[k, i, j].astype(F32)
        sq = xf * xf
        ssq[rows, :] += (sq[:, 0:128] + sq[:, 128:256]) + (sq[:, 256:384] + sq[:, 384:512])
        g4 = gain_ref[s]
        g = jnp.concatenate([g4[t : t + 1, :] for t in range(4)], axis=1)
        acc[rows, :] += _dot((xf * g).astype(BF16), wq[pl.ds(pl.multiple_of(s * HC, HC), HC), :])

    def query_blocks(n, place):
        def body(t, carry):
            i, j = place(t // 2)
            query_block(t % 2, i, j)
            return carry

        lax.fori_loop(0, 2 * n, body, 0)

    table[retr] = reqs[...]
    for o in ORDER:
        req_msg[o].wait_recv()
    to_smem = pltpu.make_async_copy(table, table_s, load_sem.at[5])
    to_smem.start()
    to_smem.wait()
    loads[2].wait()
    def parity(o):
        return (x if o == 4 else z) % 2

    def share_msg(o):
        at = pl.ds(2 * peer_from(o) + parity(o), 1)
        step = 1 - 2 * ((parity(o) + c) % 2)
        return pltpu.make_async_remote_copy(
            fetched.at[at], fetched.at[at], share_send.at[o - 4], share_recv.at[o - 4],
            device_id=device(step, 0, 0, 0) if o == 4 else device(0, 0, step, 0),
            device_id_type=MESH,
        )

    pool_msg = {}
    for o in [*ORDER, 0]:
        dy, dc = RET[o]
        to = (y + dy) % 4 * 2 + (c + dc) % 2
        first, second, seen = I32(0), I32(0), I32(0)
        for n in range(16):
            hit = table_s[to, n % 2, n // 2] == retr
            slot = table_s[to, 2 + n % 2, n // 2]
            first = jnp.where(hit & (seen == 0), slot, first)
            second = jnp.where(hit & (seen == 1), slot, second)
            seen = seen + jnp.where(hit, 1, 0)
        if o == 0:
            fetched[2 * retr] = pool[first]
            fetched[2 * retr + 1] = pool[second]
            continue
        picked[2 * o] = pool[first]
        picked[2 * o + 1] = pool[second]
        n, skip = (1, parity(o)) if dy == 2 else (2, 0)
        pool_msg[o] = pltpu.make_async_remote_copy(
            picked.at[pl.ds(2 * o + skip, n)], fetched.at[pl.ds(2 * retr + skip, n)],
            pool_send.at[o], pool_recv.at[o],
            device_id=device(0, dy, 0, dc), device_id_type=MESH,
        )
        if o in EARLY:
            pool_msg[o].start()
    mine = [table_s[retr, n % 2, n // 2] for n in range(16)]
    for n in range(16):
        before = I32(0)
        for m in range(n):
            before = before + jnp.where(mine[m] == mine[n], 1, 0)
        place_s[n] = 2 * mine[n] + before

    loads[3].wait()
    query_blocks(1, lambda t: (0, 0))

    for k in range(2):
        came(k, 1, 0)
        go(k, 3, 0, 0)
        go(k, 1, 1)
        go(k, 1, 2)
        came(k, 2, 0)
        go(k, 3, 0, 1)
        go(k, 2, 1)
        go(k, 2, 2)
    query_blocks(2, lambda t: (1 + t, 0))

    for msg in kv_msg:
        msg.wait_recv()

    def assemble(s, carry):
        part = kvrecv[s].astype(F32)
        w32[pl.ds(pl.multiple_of(s * EROWS, 8), EROWS), :] = part[:EROWS]
        return carry

    lax.fori_loop(0, 16, assemble, 0)
    wkv[c, :, pl.ds(pl.multiple_of(y * DH, DH), DH)] = w32[...].astype(BF16)

    def weight_part(dy, dc):
        return wkv.at[(c + dc) % 2, :, pl.ds(pl.multiple_of((y - dy + 4) % 4 * DH, DH), DH)]

    def weight_on(h):
        rows, cols = pl.ds(h * (ENC // 2), ENC // 2), pl.ds(pl.multiple_of((y + (3, 1)[h]) % 4 * DH, DH), DH)
        part = wkv.at[c, rows, cols]
        return pltpu.make_async_remote_copy(
            part, part, won_send.at[h], won_recv.at[h],
            device_id=device(0, (1, -1)[h], 0, 0), device_id_type=MESH,
        )

    def weight_msg(o):
        dy, dc = RET[o]
        if dc:
            return pltpu.make_async_remote_copy(
                weight_part(dy, 0), weight_part(dy, 0), wy_send.at[o], wy_recv.at[o],
                device_id=device(0, 0, 0, 1), device_id_type=MESH,
            )
        return pltpu.make_async_remote_copy(
            weight_part(0, 0), weight_part(0, 0), wy_send.at[o], wy_recv.at[o],
            device_id=device(0, dy, 0, 0), device_id_type=MESH,
        )

    wy_msg = {}

    def weight_go(o):
        wy_msg[o] = weight_msg(o)
        wy_msg[o].start()

    for o in (2, 6, 1):
        weight_go(o)
    for o in LATE:
        pool_msg[o].start()

    for k in range(2):
        came(k, 0, 1)
        go(k, 0, 3, 0)
        came(k, 0, 2)
        go(k, 0, 3, 1)
    query_blocks(2, lambda t: (0, 1 + t))
    for k in range(2):
        came(k, 3, 0, 0)
        came(k, 3, 0, 1)
        go(k, 3, 1)
        go(k, 3, 2)
    query_blocks(1, lambda t: (3, 0))
    for i in (1, 2):
        for k in range(2):
            came(k, i, 1)
            go(k, i, 3, 0)
            came(k, i, 2)
            go(k, i, 3, 1)
    query_blocks(4, lambda t: (1 + t // 2, 1 + t % 2))

    for o in (4, 5):
        pool_msg[o].wait_recv()
        share_msg(o).start()
    for k in range(2):
        came(k, 0, 3, 0)
        came(k, 0, 3, 1)
    query_blocks(1, lambda t: (0, 3))
    for h in range(2):
        wy_msg[(2, 6)[h]].wait_recv()
        weight_on(h).start()
        weight_go((3, 7)[h])
    for o in LAST:
        pool_msg[o].start()
    for k in range(2):
        came(k, 3, 1)
        go(k, 3, 3, 0)
        came(k, 3, 2)
        go(k, 3, 3, 1)
    query_blocks(2, lambda t: (3, 1 + t))
    for h in range(2):
        weight_on(h).wait_recv()
    weight_go(5)

    def kv_block(r):
        ctx = fetched[pl.ds(2 * r, 2)].reshape(2 * NL, ENC)
        turned = _dot(ctx, wkv[0]).astype(BF16).T
        keys[2 * r] = turned[:, :NL]
        keys[2 * r + 1] = turned[:, NL:]
        values[pl.ds(2 * r, 2)] = _dot(ctx, wkv[1]).astype(BF16).reshape(2, NL, HC)


    def kv_blocks(sources):
        def body(t, carry):
            r = sources[0]
            for n in range(1, len(sources)):
                r = jnp.where(t == n, sources[n], r)
            kv_block(r)
            return carry

        lax.fori_loop(0, len(sources), body, 0)

    for o in (1, 3, 5, 7):
        wy_msg[o].wait_recv()
    for o in (1, 2, 6):
        pool_msg[o].wait_recv()
    kv_blocks((retr, *(peer_from(o) for o in (1, 2, 6))))
    for k in range(2):
        for i in (1, 2):
            came(k, i, 3, 0)
            came(k, i, 3, 1)
    query_blocks(2, lambda t: (1 + t, 3))
    for o in (4, 5):
        share_msg(o).wait_recv()
    kv_blocks((peer_from(4), peer_from(5)))
    for o in (3, 7):
        pool_msg[o].wait_recv()
    kv_blocks((peer_from(3), peer_from(7)))

    def span(n, carry):
        rows = pl.ds(pl.multiple_of(n * SPAN, SPAN), SPAN)
        mean = jnp.sum(ssq[rows, :], axis=1, keepdims=True) * (1.0 / D)
        scale = lax.rsqrt(mean + 1e-05) * DH**-0.5
        j0, j1 = place_s[2 * n], place_s[2 * n + 1]
        for h in range(4):
            cols = slice(h * DH, (h + 1) * DH)
            q = (acc[rows, cols] * scale).astype(BF16)
            s0, s1 = _dot(q, keys[j0, cols, :]), _dot(q, keys[j1, cols, :])
            top = jnp.max(jnp.maximum(s0, s1), axis=1, keepdims=True)
            e0, e1 = jnp.exp(s0 - top), jnp.exp(s1 - top)
            weigh = 1.0 / jnp.sum(e0 + e1, axis=1, keepdims=True)
            o = _dot(e0.astype(BF16), values[j0, :, cols]) + _dot(e1.astype(BF16), values[j1, :, cols])
            att[rows, cols] = (o * weigh).astype(BF16)
        return carry

    loads[4].wait()

    def block(k, a, b):
        s = column(k, a, b)
        return _dot(
            att[pl.ds(pl.multiple_of(k * HALF, HALF), HALF), :],
            wo[:, pl.ds(pl.multiple_of(s * HC, HC), HC)],
        )

    def one_h(k, i, h):
        return pltpu.make_async_remote_copy(
            send1.at[k, i, 0, pl.ds(h * QUART, QUART)], recv1h.at[k, i, h],
            rs1h_send.at[k, i, h], rs1h_recv.at[k, i, h],
            device_id=along(k, 2, 1 if h == 0 else -1), device_id_type=MESH,
        )

    def one(k, i, d):
        return pltpu.make_async_remote_copy(
            send1.at[k, i, 1 + d], recv1.at[k, i, d], rs1_send.at[k, i, d], rs1_recv.at[k, i, d],
            device_id=along(k, 2, 1 if d == 0 else -1), device_id_type=MESH,
        )

    def two_h(k, h):
        return pltpu.make_async_remote_copy(
            send2.at[k, 0, pl.ds(h * QUART, QUART)], recv2h.at[k, h],
            rs2_send.at[k, h], rs2_recv.at[k, h],
            device_id=along(k, 1, 1 if h == 0 else -1), device_id_type=MESH,
        )

    def two(k, d):
        return pltpu.make_async_remote_copy(
            send2.at[k, 1 + d], recv2.at[k, d], rs2_send.at[k, 2 + d], rs2_recv.at[k, 2 + d],
            device_id=along(k, 1, 1 if d == 0 else -1), device_id_type=MESH,
        )

    FAR = (3, 1, 2, 0)
    def far(k, i):
        send1[k, i, 0] = block(k, STEP[i], 2).astype(BF16)
        for h in range(2):
            one_h(k, i, h).start()

    for k in range(2):
        came(k, 3, 3, 0)
        came(k, 3, 3, 1)
        query_block(k, 3, 3)
        lax.fori_loop(4 * k, 4 * k + 4, span, 0, unroll=4)
        far(k, 3)
    for k in range(2):
        far(k, 1)
    def to_neighbours(i):
        for k in range(2):
            for d in range(2):
                part = block(k, STEP[i], 1 if d == 0 else -1)
                one_h(k, i, d).wait_recv()
                at = pl.ds(d * QUART, QUART)
                rest = pl.ds((1 - d) * QUART, QUART)
                got = recv1h[k, i, d].astype(F32)
                send1[k, i, 1 + d, at] = (part[d * QUART : (d + 1) * QUART] + got).astype(BF16)
                send1[k, i, 1 + d, rest] = part[(1 - d) * QUART : (2 - d) * QUART].astype(BF16)
                one(k, i, d).start()
    def across(i):
        for k in range(2):
            total = acc[pl.ds(k * HALF, HALF), :] if i == 0 else block(k, STEP[i], 0)
            for d in range(2):
                one(k, i, d).wait_recv()
            total = total + recv1[k, i, 0].astype(F32) + recv1[k, i, 1].astype(F32)
            if i == 3:
                send2[k, 0] = total.astype(BF16)
                for h in range(2):
                    two_h(k, h).start()
            elif i:
                d = i - 1
                two_h(k, d).wait_recv()
                at = pl.ds(d * QUART, QUART)
                rest = pl.ds((1 - d) * QUART, QUART)
                got = recv2h[k, d].astype(F32)
                send2[k, 1 + d, at] = (total[d * QUART : (d + 1) * QUART] + got).astype(BF16)
                send2[k, 1 + d, rest] = total[(1 - d) * QUART : (2 - d) * QUART].astype(BF16)
                two(k, d).start()
            else:
                for d in range(2):
                    two(k, d).wait_recv()
                total = total + recv2[k, 0].astype(F32) + recv2[k, 1].astype(F32)
                out_ref[pl.ds(k * HALF, HALF), :] = total.astype(BF16)

    to_neighbours(3)
    for k in range(2):
        far(k, 2)
    to_neighbours(1)
    across(3)
    for k in range(2):
        far(k, 0)
    to_neighbours(2)
    across(1)
    to_neighbours(0)
    for k in range(2):
        acc[pl.ds(k * HALF, HALF), :] = slots[k, 0, 0].astype(F32) + block(k, 0, 0)
    across(2)
    across(0)

    for msg in started:
        msg.wait_send()
    for msg in kv_msg:
        msg.wait_send()
    for o in ORDER:
        req_msg[o].wait_send()
        pool_msg[o].wait_send()
        if o != 4:
            wy_msg[o].wait_send()
    for o in (4, 5):
        share_msg(o).wait_send()
        weight_on(o - 4).wait_send()
    for k in range(2):
        for i in range(4):
            for d in range(2):
                one_h(k, i, d).wait_send()
                one(k, i, d).wait_send()
        for d in range(2):
            two_h(k, d).wait_send()
            two(k, d).wait_send()


def on_device(
    tokens, norm_gain, query_weight, kv_weight, out_weight, neighbour_pool, neighbour_shard, neighbour_slot
):
    gain = norm_gain.reshape(16, 4, 128)
    vmem, hbm = pl.BlockSpec(memory_space=pltpu.VMEM), pl.BlockSpec(memory_space=pl.ANY)
    dma = pltpu.SemaphoreType.DMA
    return pl.pallas_call(
        kernel,
        out_shape=jax.ShapeDtypeStruct((ROWS, HC), BF16),
        in_specs=[hbm] * 8,
        out_specs=vmem,
        scratch_shapes=[
            pltpu.VMEM((2, 4, 4, HALF, HC), BF16),
            pltpu.VMEM((D, HC), BF16),
            pltpu.VMEM((ROWS, HC), F32),
            pltpu.VMEM((ROWS, 128), F32),
            pltpu.VMEM((16, NL, ENC), BF16),
            pltpu.VMEM((16, NL, ENC), BF16),
            pltpu.VMEM((16, NL, ENC), BF16),
            pltpu.VMEM((16, HC, NL), BF16),
            pltpu.VMEM((16, NL, HC), BF16),
            pltpu.VMEM((16, EROWS, 2, DH), BF16),
            pltpu.VMEM((16, EPAD, DH), BF16),
            pltpu.VMEM((16, EPAD, DH), BF16),
            pltpu.VMEM((ENC, DH), F32),
            pltpu.VMEM((2, ENC, HC), BF16),
            pltpu.VMEM((8, 128), I32),
            pltpu.VMEM((8, 8, 128), I32),
            pltpu.SMEM((8, 8, 128), I32),
            pltpu.SMEM((16,), I32),
            pltpu.VMEM((ROWS, HC), BF16),
            pltpu.VMEM((HC, D), BF16),
            pltpu.VMEM((2, 4, 3, HALF, HC), BF16),
            pltpu.VMEM((2, 4, 2, QUART, HC), BF16),
            pltpu.VMEM((2, 4, 2, HALF, HC), BF16),
            pltpu.VMEM((2, 3, HALF, HC), BF16),
            pltpu.VMEM((2, 2, QUART, HC), BF16),
            pltpu.VMEM((2, 2, HALF, HC), BF16),
            pltpu.VMEM((16, 4, 128), F32),
            pltpu.VMEM((2, 8), I32),
            pltpu.VMEM((2, 8), I32),
            dma((9,)), dma((16,)), dma((2, 4, 4, 2)), dma((2, 4, 4, 2)), dma((8,)), dma((8,)),
            dma((16,)), dma((16,)), dma((8,)), dma((8,)), dma((8,)), dma((8,)), dma((2,)), dma((2,)), dma((2,)), dma((2,)),
            dma((2, 4, 2)), dma((2, 4, 2)), dma((2, 4, 2)), dma((2, 4, 2)), dma((2, 4)), dma((2, 4)),
        ],
        compiler_params=pltpu.CompilerParams(
            collective_id=0, has_side_effects=True, vmem_limit_bytes=62 << 20
        ),
        cost_estimate=pl.CostEstimate(
            flops=13_000_000_000, bytes_accessed=24_000_000, transcendentals=600_000
        ),
        name="retro_block",
    )(tokens, gain, neighbour_shard.T, neighbour_slot.T, query_weight, kv_weight, out_weight, neighbour_pool)


def solution(mesh):
    return jax.shard_map(
        on_device,
        mesh=mesh,
        in_specs=(
            P("retr", "store"),
            P(),
            P(None, "store"),
            P("store", None, None),
            P("store", None),
            P("retr", None, None),
            P("retr", None),
            P("retr", None),
        ),
        out_specs=P("retr", "store"),
        check_vma=False,
    )
```

```python
import jax
import jax.numpy as jnp
from jax import lax
from jax.experimental import pallas as pl
from jax.experimental.pallas import tpu as pltpu
from jax.sharding import PartitionSpec as P

MESH = pl.DeviceIdType.MESH
BF16, F32, I32 = jnp.bfloat16, jnp.float32, jnp.int32

DH, ENC, SPAN, NL, NEIGH = 128, 896, 64, 128, 2
D, HC, ROWS, HALF, QUART = 8192, 512, 512, 256, 128
EROWS, EPAD = 56, 64
STEP = (0, 1, -1, 2)


def _dot(a, b):
    return jnp.dot(a, b, preferred_element_type=F32)


def kernel(
    tok_ref, gain_hbm, shard_hbm, slot_hbm, wq_hbm, kvw_hbm, wo_hbm, pool_hbm, out_ref,
    slots, wq, acc, ssq, pool, picked, fetched, keys, values, kvraw, kvsend, kvrecv, w32, wkv,
    reqs, table, table_s, place_s, att, wo, send1, recv1h, recv1, send2, recv2h, recv2,
    gain_ref, shard_ref, slot_ref, load_sem, raw_sem, ag_send, ag_recv, req_send, req_recv, kv_send, kv_recv,
    wy_send, wy_recv, pool_send, pool_recv, share_send, share_recv, won_send, won_recv, rs1h_send, rs1h_recv, rs1_send, rs1_recv,
    rs2_send, rs2_recv,
):
    retr, store = lax.axis_index("retr"), lax.axis_index("store")
    x, z = store // 4, store % 4
    y, c = retr // 2, retr % 2

    def device(dx, dy, dz, dc):
        return ((y + dy + 4) % 4 * 2 + (c + dc) % 2, (x + dx + 4) % 4 * 4 + (z + dz + 4) % 4)

    def along(kind, axis, step):
        return device(step, 0, 0, 0) if (kind == 0) == (axis == 1) else device(0, 0, step, 0)

    def column(kind, a, b):
        dx = jnp.where(kind == 0, a, b)
        dz = jnp.where(kind == 0, b, a)
        return (x + dx + 4) % 4 * 4 + (z + dz + 4) % 4

    def offset(i):
        return jnp.where(i == 0, 0, jnp.where(i == 1, 1, jnp.where(i == 2, -1, 2)))

    loads = [
        pltpu.make_async_copy(tok_ref.at[pl.ds(0, HALF)], slots.at[0, 0, 0], load_sem.at[0]),
        pltpu.make_async_copy(tok_ref.at[pl.ds(HALF, HALF)], slots.at[1, 0, 0], load_sem.at[1]),
        pltpu.make_async_copy(pool_hbm, pool, load_sem.at[2]),
        pltpu.make_async_copy(wq_hbm, wq, load_sem.at[3]),
        pltpu.make_async_copy(wo_hbm, wo, load_sem.at[4]),
    ]
    small = [
        pltpu.make_async_copy(shard_hbm, shard_ref, load_sem.at[6]),
        pltpu.make_async_copy(slot_hbm, slot_ref, load_sem.at[7]),
        pltpu.make_async_copy(gain_hbm, gain_ref, load_sem.at[8]),
    ]
    for copy in [*small, loads[0], loads[1]]:
        copy.start()
    barrier = pltpu.get_barrier_semaphore()
    peers = [(dx, 0, dz, 0) for dx in STEP for dz in STEP if dx or dz]
    peers += [(0, dy, 0, dc) for dy in STEP for dc in (0, 1) if dy or dc]
    for peer in sorted(peers, key=lambda p: -sum(map(abs, p))):
        pl.semaphore_signal(barrier, inc=1, device_id=device(*peer), device_id_type=MESH)
    raws = [
        pltpu.make_async_copy(
            kvw_hbm.at[:, :, pl.ds(s * HC + y * DH, DH)], kvraw.at[s], raw_sem.at[s]
        )
        for s in range(16)
    ]
    for copy in raws:
        copy.start()
    for copy in loads[2:]:
        copy.start()
    reqs[...] = jnp.zeros((8, 128), I32)
    for copy in small:
        copy.wait()
    reqs[0:2, 0:8] = shard_ref[...]
    reqs[2:4, 0:8] = slot_ref[...]

    pl.semaphore_wait(barrier, 22)

    RET = [(o // 2, o % 2) for o in range(8)]
    EARLY, LATE, LAST = [4, 5], [2, 6, 1], [3, 7]
    ORDER = EARLY + LATE + LAST

    def peer_from(o):
        dy, dc = RET[o]
        return (y - dy + 4) % 4 * 2 + (c + dc) % 2

    def gather_msg(k, i, j, h):
        axis = 2 if j else 1
        move = j if j else i
        if move == 3:
            src_move, step, half = (1, -1, 0) if h == 0 else (2, 1, 1)
            src = (i, src_move) if j else (src_move, 0)
            rows = pl.ds(half * QUART, QUART)
            return pltpu.make_async_remote_copy(
                slots.at[k, src[0], src[1], rows], slots.at[k, i, j, rows],
                ag_send.at[k, i, j, h], ag_recv.at[k, i, j, h],
                device_id=along(k, axis, step), device_id_type=MESH,
            )
        src = (i, 0) if j else (0, 0)
        step = -1 if move == 1 else 1
        return pltpu.make_async_remote_copy(
            slots.at[k, src[0], src[1]], slots.at[k, i, j],
            ag_send.at[k, i, j, 0], ag_recv.at[k, i, j, 0],
            device_id=along(k, axis, step), device_id_type=MESH,
        )

    started = []

    def go(k, i, j, h=0):
        msg = gather_msg(k, i, j, h)
        msg.start()
        started.append(msg)

    def came(k, i, j, h=0):
        gather_msg(k, i, j, h).wait_recv()

    loads[0].wait()
    loads[1].wait()
    for k in range(2):
        go(k, 1, 0)
        go(k, 2, 0)
    req_msg = {}
    for o in ORDER:
        req_msg[o] = pltpu.make_async_remote_copy(
            reqs, table.at[retr], req_send.at[o], req_recv.at[o],
            device_id=device(0, RET[o][0], 0, RET[o][1]), device_id_type=MESH,
        )
        req_msg[o].start()
    for k in range(2):
        go(k, 0, 1)
        go(k, 0, 2)

    for copy in raws:
        copy.wait()

    def split(s, carry):
        raw = kvraw[s].astype(F32)
        one = jnp.where(c == 0, raw[:, 0, :], raw[:, 1, :])
        kvsend[s] = jnp.concatenate([one, jnp.zeros((EPAD - EROWS, DH), F32)], axis=0).astype(BF16)
        return carry

    lax.fori_loop(0, 16, split, 0)
    kv_msg = []
    for o in range(1, 16):
        to = (store + o) % 16
        msg = pltpu.make_async_remote_copy(
            kvsend.at[to], kvrecv.at[store], kv_send.at[o], kv_recv.at[o],
            device_id=(retr, to), device_id_type=MESH,
        )
        msg.start()
        kv_msg.append(msg)
    kvrecv[store] = kvsend[store]

    acc[...] = jnp.zeros((ROWS, HC), F32)
    ssq[...] = jnp.zeros((ROWS, 128), F32)

    def query_block(k, i, j):
        s = column(k, offset(i), offset(j))
        rows = pl.ds(k * HALF, HALF)
        xf = slots[k, i, j].astype(F32)
        sq = xf * xf
        ssq[rows, :] += (sq[:, 0:128] + sq[:, 128:256]) + (sq[:, 256:384] + sq[:, 384:512])
        g4 = gain_ref[s]
        g = jnp.concatenate([g4[t : t + 1, :] for t in range(4)], axis=1)
        acc[rows, :] += _dot((xf * g).astype(BF16), wq[pl.ds(pl.multiple_of(s * HC, HC), HC), :])

    def query_blocks(n, place):
        def body(t, carry):
            i, j = place(t // 2)
            query_block(t % 2, i, j)
            return carry

        lax.fori_loop(0, 2 * n, body, 0)

    table[retr] = reqs[...]
    for o in ORDER:
        req_msg[o].wait_recv()
    to_smem = pltpu.make_async_copy(table, table_s, load_sem.at[5])
    to_smem.start()
    to_smem.wait()
    loads[2].wait()
    def parity(o):
        return (x if o == 4 else z) % 2

    def share_msg(o):
        at = pl.ds(2 * peer_from(o) + parity(o), 1)
        step = 1 - 2 * ((parity(o) + c) % 2)
        return pltpu.make_async_remote_copy(
            fetched.at[at], fetched.at[at], share_send.at[o - 4], share_recv.at[o - 4],
            device_id=device(step, 0, 0, 0) if o == 4 else device(0, 0, step, 0),
            device_id_type=MESH,
        )

    pool_msg = {}
    for o in [*ORDER, 0]:
        dy, dc = RET[o]
        to = (y + dy) % 4 * 2 + (c + dc) % 2
        first, second, seen = I32(0), I32(0), I32(0)
        for n in range(16):
            hit = table_s[to, n % 2, n // 2] == retr
            slot = table_s[to, 2 + n % 2, n // 2]
            first = jnp.where(hit & (seen == 0), slot, first)
            second = jnp.where(hit & (seen == 1), slot, second)
            seen = seen + jnp.where(hit, 1, 0)
        if o == 0:
            fetched[2 * retr] = pool[first]
            fetched[2 * retr + 1] = pool[second]
            continue
        picked[2 * o] = pool[first]
        picked[2 * o + 1] = pool[second]
        n, skip = (1, parity(o)) if dy == 2 else (2, 0)
        pool_msg[o] = pltpu.make_async_remote_copy(
            picked.at[pl.ds(2 * o + skip, n)], fetched.at[pl.ds(2 * retr + skip, n)],
            pool_send.at[o], pool_recv.at[o],
            device_id=device(0, dy, 0, dc), device_id_type=MESH,
        )
        if o in EARLY:
            pool_msg[o].start()
    mine = [table_s[retr, n % 2, n // 2] for n in range(16)]
    for n in range(16):
        before = I32(0)
        for m in range(n):
            before = before + jnp.where(mine[m] == mine[n], 1, 0)
        place_s[n] = 2 * mine[n] + before

    loads[3].wait()
    query_blocks(1, lambda t: (0, 0))

    for k in range(2):
        came(k, 1, 0)
        go(k, 3, 0, 0)
        go(k, 1, 1)
        go(k, 1, 2)
        came(k, 2, 0)
        go(k, 3, 0, 1)
        go(k, 2, 1)
        go(k, 2, 2)
    query_blocks(2, lambda t: (1 + t, 0))

    for msg in kv_msg:
        msg.wait_recv()

    def assemble(s, carry):
        part = kvrecv[s].astype(F32)
        w32[pl.ds(pl.multiple_of(s * EROWS, 8), EROWS), :] = part[:EROWS]
        return carry

    lax.fori_loop(0, 16, assemble, 0)
    wkv[c, :, pl.ds(pl.multiple_of(y * DH, DH), DH)] = w32[...].astype(BF16)

    def weight_part(dy, dc):
        return wkv.at[(c + dc) % 2, :, pl.ds(pl.multiple_of((y - dy + 4) % 4 * DH, DH), DH)]

    def weight_on(h):
        rows, cols = pl.ds(h * (ENC // 2), ENC // 2), pl.ds(pl.multiple_of((y + (3, 1)[h]) % 4 * DH, DH), DH)
        part = wkv.at[c, rows, cols]
        return pltpu.make_async_remote_copy(
            part, part, won_send.at[h], won_recv.at[h],
            device_id=device(0, (1, -1)[h], 0, 0), device_id_type=MESH,
        )

    def weight_msg(o):
        dy, dc = RET[o]
        if dc:
            return pltpu.make_async_remote_copy(
                weight_part(dy, 0), weight_part(dy, 0), wy_send.at[o], wy_recv.at[o],
                device_id=device(0, 0, 0, 1), device_id_type=MESH,
            )
        return pltpu.make_async_remote_copy(
            weight_part(0, 0), weight_part(0, 0), wy_send.at[o], wy_recv.at[o],
            device_id=device(0, dy, 0, 0), device_id_type=MESH,
        )

    wy_msg = {}

    def weight_go(o):
        wy_msg[o] = weight_msg(o)
        wy_msg[o].start()

    for o in (2, 6, 1):
        weight_go(o)
    for o in LATE:
        pool_msg[o].start()

    for k in range(2):
        came(k, 0, 1)
        go(k, 0, 3, 0)
        came(k, 0, 2)
        go(k, 0, 3, 1)
    query_blocks(2, lambda t: (0, 1 + t))
    for k in range(2):
        came(k, 3, 0, 0)
        came(k, 3, 0, 1)
        go(k, 3, 1)
        go(k, 3, 2)
    query_blocks(1, lambda t: (3, 0))
    for i in (1, 2):
        for k in range(2):
            came(k, i, 1)
            go(k, i, 3, 0)
            came(k, i, 2)
            go(k, i, 3, 1)
    query_blocks(4, lambda t: (1 + t // 2, 1 + t % 2))

    for o in (4, 5):
        pool_msg[o].wait_recv()
        share_msg(o).start()
    for k in range(2):
        came(k, 0, 3, 0)
        came(k, 0, 3, 1)
    query_blocks(1, lambda t: (0, 3))
    for h in range(2):
        wy_msg[(2, 6)[h]].wait_recv()
        weight_on(h).start()
        weight_go((3, 7)[h])
    for o in LAST:
        pool_msg[o].start()
    for k in range(2):
        came(k, 3, 1)
        go(k, 3, 3, 0)
        came(k, 3, 2)
        go(k, 3, 3, 1)
    query_blocks(2, lambda t: (3, 1 + t))
    for h in range(2):
        weight_on(h).wait_recv()
    weight_go(5)

    def kv_block(r):
        ctx = fetched[pl.ds(2 * r, 2)].reshape(2 * NL, ENC)
        turned = _dot(ctx, wkv[0]).astype(BF16).T
        keys[2 * r] = turned[:, :NL]
        keys[2 * r + 1] = turned[:, NL:]
        values[pl.ds(2 * r, 2)] = _dot(ctx, wkv[1]).astype(BF16).reshape(2, NL, HC)


    def kv_blocks(sources):
        def body(t, carry):
            r = sources[0]
            for n in range(1, len(sources)):
                r = jnp.where(t == n, sources[n], r)
            kv_block(r)
            return carry

        lax.fori_loop(0, len(sources), body, 0)

    for o in (1, 3, 5, 7):
        wy_msg[o].wait_recv()
    for o in (1, 2, 6):
        pool_msg[o].wait_recv()
    kv_blocks((retr, *(peer_from(o) for o in (1, 2, 6))))
    for k in range(2):
        for i in (1, 2):
            came(k, i, 3, 0)
            came(k, i, 3, 1)
    query_blocks(2, lambda t: (1 + t, 3))
    for o in (3, 7):
        pool_msg[o].wait_recv()
    kv_blocks((peer_from(3), peer_from(7)))
    for o in (4, 5):
        share_msg(o).wait_recv()
    kv_blocks((peer_from(4), peer_from(5)))

    def span(n, carry):
        rows = pl.ds(pl.multiple_of(n * SPAN, SPAN), SPAN)
        mean = jnp.sum(ssq[rows, :], axis=1, keepdims=True) * (1.0 / D)
        scale = lax.rsqrt(mean + 1e-05) * DH**-0.5
        j0, j1 = place_s[2 * n], place_s[2 * n + 1]
        for h in range(4):
            cols = slice(h * DH, (h + 1) * DH)
            q = (acc[rows, cols] * scale).astype(BF16)
            s0, s1 = _dot(q, keys[j0, cols, :]), _dot(q, keys[j1, cols, :])
            top = jnp.max(jnp.maximum(s0, s1), axis=1, keepdims=True)
            e0, e1 = jnp.exp(s0 - top), jnp.exp(s1 - top)
            weigh = 1.0 / jnp.sum(e0 + e1, axis=1, keepdims=True)
            o = _dot(e0.astype(BF16), values[j0, :, cols]) + _dot(e1.astype(BF16), values[j1, :, cols])
            att[rows, cols] = (o * weigh).astype(BF16)
        return carry

    loads[4].wait()

    def block(k, a, b):
        s = column(k, a, b)
        return _dot(
            att[pl.ds(pl.multiple_of(k * HALF, HALF), HALF), :],
            wo[:, pl.ds(pl.multiple_of(s * HC, HC), HC)],
        )

    def one_h(k, i, h):
        return pltpu.make_async_remote_copy(
            send1.at[k, i, 0, pl.ds(h * QUART, QUART)], recv1h.at[k, i, h],
            rs1h_send.at[k, i, h], rs1h_recv.at[k, i, h],
            device_id=along(k, 2, 1 if h == 0 else -1), device_id_type=MESH,
        )

    def one(k, i, d):
        return pltpu.make_async_remote_copy(
            send1.at[k, i, 1 + d], recv1.at[k, i, d], rs1_send.at[k, i, d], rs1_recv.at[k, i, d],
            device_id=along(k, 2, 1 if d == 0 else -1), device_id_type=MESH,
        )

    def two_h(k, h):
        return pltpu.make_async_remote_copy(
            send2.at[k, 0, pl.ds(h * QUART, QUART)], recv2h.at[k, h],
            rs2_send.at[k, h], rs2_recv.at[k, h],
            device_id=along(k, 1, 1 if h == 0 else -1), device_id_type=MESH,
        )

    def two(k, d):
        return pltpu.make_async_remote_copy(
            send2.at[k, 1 + d], recv2.at[k, d], rs2_send.at[k, 2 + d], rs2_recv.at[k, 2 + d],
            device_id=along(k, 1, 1 if d == 0 else -1), device_id_type=MESH,
        )

    FAR = (3, 1, 2, 0)
    def far(k, i):
        send1[k, i, 0] = block(k, STEP[i], 2).astype(BF16)
        for h in range(2):
            one_h(k, i, h).start()

    for k in range(2):
        came(k, 3, 3, 0)
        came(k, 3, 3, 1)
        query_block(k, 3, 3)
        lax.fori_loop(4 * k, 4 * k + 4, span, 0, unroll=4)
        far(k, 3)
    for k in range(2):
        far(k, 1)
    def to_neighbours(i):
        for k in range(2):
            for d in range(2):
                part = block(k, STEP[i], 1 if d == 0 else -1)
                one_h(k, i, d).wait_recv()
                at = pl.ds(d * QUART, QUART)
                rest = pl.ds((1 - d) * QUART, QUART)
                got = recv1h[k, i, d].astype(F32)
                send1[k, i, 1 + d, at] = (part[d * QUART : (d + 1) * QUART] + got).astype(BF16)
                send1[k, i, 1 + d, rest] = part[(1 - d) * QUART : (2 - d) * QUART].astype(BF16)
                one(k, i, d).start()
    def result(k):
        rows = pl.ds(k * HALF, HALF)
        return pltpu.make_async_copy(att.at[rows], out_ref.at[rows], load_sem.at[k])

    def across(i):
        for k in range(2):
            total = acc[pl.ds(k * HALF, HALF), :] if i == 0 else block(k, STEP[i], 0)
            for d in range(2):
                one(k, i, d).wait_recv()
            total = total + recv1[k, i, 0].astype(F32) + recv1[k, i, 1].astype(F32)
            if i == 3:
                send2[k, 0] = total.astype(BF16)
                for h in range(2):
                    two_h(k, h).start()
            elif i:
                d = i - 1
                two_h(k, d).wait_recv()
                at = pl.ds(d * QUART, QUART)
                rest = pl.ds((1 - d) * QUART, QUART)
                got = recv2h[k, d].astype(F32)
                send2[k, 1 + d, at] = (total[d * QUART : (d + 1) * QUART] + got).astype(BF16)
                send2[k, 1 + d, rest] = total[(1 - d) * QUART : (2 - d) * QUART].astype(BF16)
                two(k, d).start()
            else:
                for d in range(2):
                    two(k, d).wait_recv()
                total = total + recv2[k, 0].astype(F32) + recv2[k, 1].astype(F32)
                att[pl.ds(k * HALF, HALF), :] = total.astype(BF16)
                result(k).start()

    to_neighbours(3)
    for k in range(2):
        far(k, 2)
    to_neighbours(1)
    across(3)
    for k in range(2):
        far(k, 0)
    to_neighbours(2)
    across(1)
    to_neighbours(0)
    for k in range(2):
        acc[pl.ds(k * HALF, HALF), :] = slots[k, 0, 0].astype(F32) + block(k, 0, 0)
    across(2)
    across(0)

    for msg in started:
        msg.wait_send()
    for msg in kv_msg:
        msg.wait_send()
    for o in ORDER:
        req_msg[o].wait_send()
        pool_msg[o].wait_send()
        if o != 4:
            wy_msg[o].wait_send()
    for o in (4, 5):
        share_msg(o).wait_send()
        weight_on(o - 4).wait_send()
    for k in range(2):
        for i in range(4):
            for d in range(2):
                one_h(k, i, d).wait_send()
                one(k, i, d).wait_send()
        for d in range(2):
            two_h(k, d).wait_send()
            two(k, d).wait_send()
    for k in range(2):
        result(k).wait()


def on_device(
    tokens, norm_gain, query_weight, kv_weight, out_weight, neighbour_pool, neighbour_shard, neighbour_slot
):
    gain = norm_gain.reshape(16, 4, 128)
    hbm = pl.BlockSpec(memory_space=pl.ANY)
    dma = pltpu.SemaphoreType.DMA
    return pl.pallas_call(
        kernel,
        out_shape=jax.ShapeDtypeStruct((ROWS, HC), BF16),
        in_specs=[hbm] * 8,
        out_specs=hbm,
        scratch_shapes=[
            pltpu.VMEM((2, 4, 4, HALF, HC), BF16),
            pltpu.VMEM((D, HC), BF16),
            pltpu.VMEM((ROWS, HC), F32),
            pltpu.VMEM((ROWS, 128), F32),
            pltpu.VMEM((16, NL, ENC), BF16),
            pltpu.VMEM((16, NL, ENC), BF16),
            pltpu.VMEM((16, NL, ENC), BF16),
            pltpu.VMEM((16, HC, NL), BF16),
            pltpu.VMEM((16, NL, HC), BF16),
            pltpu.VMEM((16, EROWS, 2, DH), BF16),
            pltpu.VMEM((16, EPAD, DH), BF16),
            pltpu.VMEM((16, EPAD, DH), BF16),
            pltpu.VMEM((ENC, DH), F32),
            pltpu.VMEM((2, ENC, HC), BF16),
            pltpu.VMEM((8, 128), I32),
            pltpu.VMEM((8, 8, 128), I32),
            pltpu.SMEM((8, 8, 128), I32),
            pltpu.SMEM((16,), I32),
            pltpu.VMEM((ROWS, HC), BF16),
            pltpu.VMEM((HC, D), BF16),
            pltpu.VMEM((2, 4, 3, HALF, HC), BF16),
            pltpu.VMEM((2, 4, 2, QUART, HC), BF16),
            pltpu.VMEM((2, 4, 2, HALF, HC), BF16),
            pltpu.VMEM((2, 3, HALF, HC), BF16),
            pltpu.VMEM((2, 2, QUART, HC), BF16),
            pltpu.VMEM((2, 2, HALF, HC), BF16),
            pltpu.VMEM((16, 4, 128), F32),
            pltpu.VMEM((2, 8), I32),
            pltpu.VMEM((2, 8), I32),
            dma((9,)), dma((16,)), dma((2, 4, 4, 2)), dma((2, 4, 4, 2)), dma((8,)), dma((8,)),
            dma((16,)), dma((16,)), dma((8,)), dma((8,)), dma((8,)), dma((8,)), dma((2,)), dma((2,)), dma((2,)), dma((2,)),
            dma((2, 4, 2)), dma((2, 4, 2)), dma((2, 4, 2)), dma((2, 4, 2)), dma((2, 4)), dma((2, 4)),
        ],
        compiler_params=pltpu.CompilerParams(
            collective_id=0, has_side_effects=True, vmem_limit_bytes=62 << 20
        ),
        cost_estimate=pl.CostEstimate(
            flops=13_000_000_000, bytes_accessed=24_000_000, transcendentals=600_000
        ),
        name="retro_block",
    )(tokens, gain, neighbour_shard.T, neighbour_slot.T, query_weight, kv_weight, out_weight, neighbour_pool)


def solution(mesh):
    return jax.shard_map(
        on_device,
        mesh=mesh,
        in_specs=(
            P("retr", "store"),
            P(),
            P(None, "store"),
            P("store", None, None),
            P("store", None),
            P("retr", None, None),
            P("retr", None),
            P("retr", None),
        ),
        out_specs=P("retr", "store"),
        check_vma=False,
    )
```
